32 devices in a mesh: dp: 2 (over x), row: 4 (over z), col: 4 (over y, core).
Axes of the slice: x: 2, y: 2, z: 4, core: 2. Of those that a mesh axis runs over, the one named last changes fastest.
Arguments:
- activations: bfloat16 [8192, 1536], P(('dp', 'row'), 'col'), may hold values from -6 to 6
- cotangent: bfloat16 [8192, 1536], P(('dp', 'row'), 'col'), may hold values from -6 to 6
- gain_one: bfloat16 [1536], P('col'), may hold values from 0.5 to 1.5
- gain_two: bfloat16 [1536], P('col'), may hold values from 0.5 to 1.5
- w_query: bfloat16 [1536, 1536], P('col', 'row'), may hold values from -0.15625 to 0.15625
- key_projection_weight: bfloat16 [1536, 512], P('col', 'row'), may hold values from -0.15625 to 0.15625
- value_projection_weight: bfloat16 [1536, 512], P('col', 'row'), may hold values from -0.15625 to 0.15625
- w_out: bfloat16 [1536, 1536], P('row', 'col'), may hold values from -0.625 to 0.625
- w_router: bfloat16 [1536, 40], P('col'), may hold values from -0.078125 to 0.078125
- w_gate: bfloat16 [40, 1536, 512], P(None, 'col', 'row'), may hold values from -0.15625 to 0.15625
- w_up: bfloat16 [40, 1536, 512], P(None, 'col', 'row'), may hold values from -0.15625 to 0.15625
- w_down: bfloat16 [40, 512, 1536], P(None, 'row', 'col'), may hold values from -1 to 1
- routes: int32 [8192, 8], P('dp'), may hold values from 0 to 39, all different within a row; in each aligned block of 4096 rows (0 to 4095, 4096 to 8191, ...) at most 1024 rows name the same one
- doc_lengths: int32 [8, 4], P('dp'), may hold values from 1 to 512, 1024 in all within a row
Outputs:
- block_out: bfloat16 [8192, 1536], P(('dp', 'row'), 'col')
- input_grad: bfloat16 [8192, 1536], P(('dp', 'row'), 'col')
- gain_one_grad: float32 [1536], P('col')
- gain_two_grad: float32 [1536], P('col')
- w_query_grad: float32 [1536, 1536], P(('col', 'dp'), 'row')
- w_key_grad: float32 [1536, 512], P(('col', 'dp'), 'row')
- w_value_grad: float32 [1536, 512], P(('col', 'dp'), 'row')
- w_out_grad: float32 [1536, 1536], P(('row', 'dp'), 'col')
- w_router_grad: float32 [1536, 40], P(('col', 'dp'))
- w_gate_grad: float32 [40, 1536, 512], P(None, ('col', 'dp'), 'row')
- w_up_grad: float32 [40, 1536, 512], P(None, ('col', 'dp'), 'row')
- w_down_grad: float32 [40, 512, 1536], P(None, 'row', ('col', 'dp'))
The draws below stay inside these ranges and needn't reach their ends.
Inputs may be any that keep to these rules, and one draw needn't show every extreme that they name: `routes`: each row names 8 different experts; within each aligned block of 4096 rows no expert is named by more than 1024 rows, a bound that some block reaches. `doc_lengths`: each row sums to 1024.
All inputs are finite; a program needn't handle non-finite values.
Results may differ from the reference program's by a relative error of at most 0.025.
Values may be sent and summed in bfloat16 or wider, within the bound.
No kernel may reach another device: no remote copies, remote signals or barrier semaphores. Data moves between devices by JAX's collectives and lax.ppermute only.
A program may use at most 512 MiB of HBM per device.

```python
import math
import jax
import jax.numpy as jnp
import numpy as np
from jax import lax

MODEL_WIDTH = 1536
QUERY_HEADS = 24
KEY_VALUE_HEADS = 8
HEAD_SIZE = 64
H = 512
E = 40
TOP = 8
SEQUENCE_LENGTH = 1024
DOCS = 4
SEQ_GROUP = 4
TOK_GROUP = 4096
CAP = 1024
TOKENS = 8192
SEQS = 8
N_DP = 2


def steps_of(own_key, shape, split, smallest, largest):
    def one(position, shards_of):
        draws = jax.random.uniform(jax.random.fold_in(jax.random.fold_in(own_key, 6), position), (shards_of,), jnp.float32, smallest / len(split), largest / len(split))
        return jnp.repeat(jnp.exp(draws), shape[position] // shards_of).reshape((-1,) + (1,) * (len(shape) - position - 1))

    level = one(*split[0])
    for cut in split[1:]:
        level = level * one(*cut)
    return level


def split_up(amount, total, most, slope):
    weights = [(1 << 20) // math.isqrt(rank ** slope) + 1 for rank in range(2, amount + 1)]
    surplus, holding = total - most - (amount - 1), [1] * (amount - 1)
    while surplus > 0:
        candidates = [i for i in range(amount - 1) if holding[i] < most]
        mass, left = sum([weights[i] for i in candidates]), surplus
        for i in candidates:
            addition = min(most - holding[i], max(1, left * weights[i] // mass), surplus)
            holding[i] = holding[i] + addition
            surplus = surplus - addition
    return np.array([most] + holding)


def uneven_parts(stream_key, amount, total, reach, skew):
    if amount == 2:
        one = jax.random.randint(stream_key, (), max(1, total - reach), min(reach, total - 1) + 1)
        return jnp.stack([one, total - one])
    tallies = jnp.asarray(split_up(amount, total, reach, skew), jnp.int32)
    twos = (amount - 1) // 2
    giver, sink = tallies[1:1 + 2 * twos:2], tallies[2:2 + 2 * twos:2]
    margin = jnp.minimum(giver - 1, reach - sink)
    passed = jax.random.randint(jax.random.fold_in(stream_key, 1), (twos,), 0, 1 << 20) % (margin + 1)
    tallies = tallies.at[1:1 + 2 * twos:2].set(giver - passed).at[2:2 + 2 * twos:2].set(sink + passed)
    return tallies[jax.random.permutation(jax.random.fold_in(stream_key, 2), amount)]


def shared_out(rng, own, number, rows, number_of, top, bound, skew):
    order = jax.random.permutation(rng, number_of)
    packed, usual = shares(number_of, rows * top, bound, skew, True), shares(number_of, rows * top, bound, skew, False)
    places = jnp.arange(number_of)

    def named(lengths, turn):
        used = int((lengths > 0).sum())
        fixed = max(1, used // 4)
        passed = fixed + (places - fixed + turn * (used - fixed)) % max(1, number_of - fixed)
        return jnp.zeros((number_of,), jnp.int32).at[order[jnp.where(places < fixed, places, passed)]].set(jnp.asarray(lengths, jnp.int32))

    lengths = jnp.where(number % 4 == 0, named(packed, number // 4), named(usual, number - number // 4 - 1))
    mixed = jax.random.permutation(jax.random.fold_in(own, 3), number_of)
    giver, taker = mixed[0:number_of // 2 * 2:2], mixed[1:number_of // 2 * 2:2]
    margin = jnp.minimum(lengths[giver] - 1, bound - lengths[taker]) // 2
    margin = jnp.where((giver == order[0]) | (taker == order[0]) | (lengths[taker] == 0), 0, jnp.maximum(margin, 0))
    passed = jax.random.randint(jax.random.fold_in(own, 4), (number_of // 2,), 0, 1 << 20) % (margin + 1)
    lengths = lengths.at[giver].add(-passed).at[taker].add(passed)
    labels = jnp.searchsorted(jnp.cumsum(lengths), jnp.arange(rows * top), side="right").astype(jnp.int32)
    table = labels.reshape(top, rows).T
    table = table[jax.random.permutation(jax.random.fold_in(own, 1), rows)]
    turn = jax.random.randint(jax.random.fold_in(own, 2), (rows, 1), 0, top)
    return jnp.take_along_axis(table, (jnp.arange(top)[None, :] + turn) % top, axis=1)


def shares(count, total, most, skew, full):
    loads = [(1 << 20) // math.isqrt(rank ** skew) + 1 for rank in range(1, count + 1)]
    largest = most if full else min(most, max(-(-total // count), total * loads[0] // sum(loads)))
    least = 1 if total - largest >= count - 1 else 0
    given, surplus = [largest] + [least] * (count - 1), total - largest - least * (count - 1)
    while surplus > 0:
        candidates = [i for i in range(1, count) if given[i] < largest] or [i for i in range(1, count) if given[i] < most]
        whole, left = sum([loads[i] for i in candidates]), surplus
        for i in candidates:
            addition = min(most - given[i], max(1, left * loads[i] // whole), surplus)
            given[i] = given[i] + addition
            surplus = surplus - addition
    return np.array(given)


def bell_draw(stream_key, extent, scale, limit, pieces=(), dtype=jnp.bfloat16):
    drawn = jax.random.normal(stream_key, extent, jnp.float32) * scale
    if len(pieces) > 0:
        drawn = steps_of(stream_key, extent, pieces, -0.22, 0.18) * drawn
    return jnp.clip(drawn, min=-limit, max=limit).astype(dtype)


def setup_inputs(seed: int = 0) -> dict:
    splits = jax.random.split(jax.random.key(seed), 15)
    activations = bell_draw(splits[0], (TOKENS, MODEL_WIDTH), 1.0, 6.0, ((0, 8), (1, 4)))
    cotangent = bell_draw(splits[1], (TOKENS, MODEL_WIDTH), 1.0, 6.0, ((0, 8), (1, 4)))
    gain_one = jnp.clip(1.0 + 0.1 * jax.random.normal(splits[2], (MODEL_WIDTH,), jnp.float32), 0.5, 1.5).astype(jnp.bfloat16)
    gain_two = jnp.clip(1.0 + 0.1 * jax.random.normal(splits[3], (MODEL_WIDTH,), jnp.float32), 0.5, 1.5).astype(jnp.bfloat16)
    w_query = bell_draw(splits[4], (MODEL_WIDTH, QUERY_HEADS * HEAD_SIZE), MODEL_WIDTH ** -0.5, 0.15625, ((0, 4), (1, 4)))
    key_projection_weight = bell_draw(splits[5], (MODEL_WIDTH, KEY_VALUE_HEADS * HEAD_SIZE), MODEL_WIDTH ** -0.5, 0.15625, ((0, 4), (1, 4)))
    value_projection_weight = bell_draw(splits[6], (MODEL_WIDTH, KEY_VALUE_HEADS * HEAD_SIZE), MODEL_WIDTH ** -0.5, 0.15625, ((0, 4), (1, 4)))
    w_out = bell_draw(splits[7], (QUERY_HEADS * HEAD_SIZE, MODEL_WIDTH), (QUERY_HEADS * HEAD_SIZE // 16) ** -0.5, 0.625, ((0, 4), (1, 4)))
    w_router = bell_draw(splits[8], (MODEL_WIDTH, E), (4 * MODEL_WIDTH) ** -0.5, 0.078125, ((0, 4),))
    w_gate = bell_draw(splits[9], (E, MODEL_WIDTH, H), MODEL_WIDTH ** -0.5, 0.15625, ((1, 4), (2, 4)))
    w_up = bell_draw(splits[10], (E, MODEL_WIDTH, H), MODEL_WIDTH ** -0.5, 0.15625, ((1, 4), (2, 4)))
    w_down = bell_draw(splits[11], (E, H, MODEL_WIDTH), (H // 16) ** -0.5, 1.0, ((1, 4), (2, 4)))
    routes_keys = jax.random.split(jax.random.fold_in(splits[12], 1), TOKENS // TOK_GROUP)
    routes_turns = jax.random.permutation(jax.random.fold_in(splits[12], 3), TOKENS // TOK_GROUP)
    routes = jax.vmap(lambda own, number: shared_out(jax.random.fold_in(splits[12], 2), own, number, TOK_GROUP, E, TOP, CAP, 1))(routes_keys, routes_turns).reshape((TOKENS, TOP))
    doc_lengths = jax.vmap(lambda own: uneven_parts(own, DOCS, SEQUENCE_LENGTH, SEQUENCE_LENGTH // 2, 2))(jax.random.split(splits[13], SEQS)).reshape((SEQS, DOCS)).astype(jnp.int32)
    return {"activations": activations, "cotangent": cotangent, "gain_one": gain_one, "gain_two": gain_two, "w_query": w_query, "key_projection_weight": key_projection_weight, "value_projection_weight": value_projection_weight, "w_out": w_out, "w_router": w_router, "w_gate": w_gate, "w_up": w_up, "w_down": w_down, "routes": routes, "doc_lengths": doc_lengths}


@jax.custom_vjp
def low(v):
    return lax.optimization_barrier(v.astype(jnp.bfloat16)).astype(jnp.float32)

@jax.custom_vjp
def low_back(v):
    return v

def low_keep(v):
    return (low(v), None)

def low_pass(kept, grad):
    return (grad,)

def back_keep(v):
    return (v, None)

def back_low(kept, grad):
    return (low(grad),)
low.defvjp(low_keep, low_pass)
low_back.defvjp(back_keep, back_low)
epsilon = 1e-06
highest_precision = lax.Precision.HIGHEST

def normalize(row_block, gain):
    mean_square = lax.optimization_barrier(jnp.mean(row_block * row_block, axis=1, keepdims=True))
    return row_block * lax.rsqrt(mean_square + epsilon) * gain

def rotate(values_in, positions):
    half_width = HEAD_SIZE // 2
    frequency = 10000.0 ** (-jnp.arange(half_width).astype(jnp.float32) / half_width)
    angles = positions.astype(jnp.float32)[:, None] * frequency[None, :]
    cosine = jnp.cos(angles)[:, None, :]
    sine_part = jnp.sin(angles)[:, None, :]
    first_half = values_in[..., :half_width]
    second = values_in[..., half_width:]
    return jnp.concatenate([first_half * cosine - second * sine_part, second * cosine + first_half * sine_part], axis=-1)

def attend_one_sequence(seq_items):
    query_matrix, projected_keys, projected_values, sequence_lengths = seq_items
    positions = jnp.arange(SEQUENCE_LENGTH).astype(jnp.int32)
    doc_ends = jnp.cumsum(sequence_lengths).astype(jnp.int32)
    doc_ids = lax.optimization_barrier(jnp.sum((positions[:, None] >= doc_ends[None, :]).astype(jnp.int32), axis=1))
    allowed = (doc_ids[:, None] == doc_ids[None, :]) & (positions[:, None] >= positions[None, :])
    grouped_queries = query_matrix.reshape(SEQUENCE_LENGTH, KEY_VALUE_HEADS, QUERY_HEADS // KEY_VALUE_HEADS, HEAD_SIZE)
    scores = jnp.einsum('qkgd,skd->kgqs', grouped_queries, projected_keys, precision=highest_precision) * HEAD_SIZE ** (-0.5)
    scores = low_back(scores)
    scores = jnp.where(allowed[None, None], scores, -1e+30)
    softmax_probs = jax.nn.softmax(scores, axis=-1)
    attention_output = jnp.einsum('kgqs,skd->qkgd', low(softmax_probs), projected_values, precision=highest_precision)
    return attention_output.reshape(SEQUENCE_LENGTH, QUERY_HEADS * HEAD_SIZE)

def layer_group(row_block, route_rows, sequence_lengths, weights):
    gain_one, gain_two, w_query, key_projection_weight, value_projection_weight, w_out, w_router, w_gate, w_up, w_down = weights
    token_count = row_block.shape[0]
    sequence_count = token_count // SEQUENCE_LENGTH
    first_normed_input = low(normalize(row_block, gain_one))
    positions = (jnp.arange(token_count) % SEQUENCE_LENGTH).astype(jnp.int32)
    query_matrix = jnp.dot(first_normed_input, w_query, precision=highest_precision).reshape(token_count, QUERY_HEADS, HEAD_SIZE)
    projected_keys = jnp.dot(first_normed_input, key_projection_weight, precision=highest_precision).reshape(token_count, KEY_VALUE_HEADS, HEAD_SIZE)
    projected_values = jnp.dot(first_normed_input, value_projection_weight, precision=highest_precision).reshape(token_count, KEY_VALUE_HEADS, HEAD_SIZE)
    query_matrix = low(rotate(low_back(query_matrix), positions))
    projected_keys = low(rotate(low_back(projected_keys), positions))
    projected_values = low(low_back(projected_values))
    attention_output = lax.map(jax.checkpoint(attend_one_sequence), (query_matrix.reshape(sequence_count, SEQUENCE_LENGTH, QUERY_HEADS, HEAD_SIZE), projected_keys.reshape(sequence_count, SEQUENCE_LENGTH, KEY_VALUE_HEADS, HEAD_SIZE), projected_values.reshape(sequence_count, SEQUENCE_LENGTH, KEY_VALUE_HEADS, HEAD_SIZE), sequence_lengths))
    attention_output = low(low_back(attention_output.reshape(token_count, QUERY_HEADS * HEAD_SIZE)))
    hidden = row_block + low_back(jnp.dot(attention_output, w_out, precision=highest_precision))
    normed_two = low(normalize(hidden, gain_two))
    logits = low_back(jnp.dot(normed_two, w_router, precision=highest_precision))
    chosen = jnp.take_along_axis(logits, route_rows, axis=1)
    gate_weights = jax.nn.softmax(chosen, axis=-1)
    flat_routes = route_rows.reshape(-1)
    onehot = (flat_routes[:, None] == jnp.arange(E).astype(jnp.int32)[None, :]).astype(jnp.int32)
    slot_index = lax.optimization_barrier(jnp.sum((jnp.cumsum(onehot, axis=0).astype(jnp.int32) - 1) * onehot, axis=1)).astype(jnp.int32)
    slot_flat = (flat_routes * CAP + slot_index).astype(jnp.int32)
    token_ids = (jnp.arange(token_count * TOP) // TOP).astype(jnp.int32)
    slot_owner = jnp.full((E * CAP,), token_count, jnp.int32).at[slot_flat].set(token_ids)
    padded = jnp.concatenate([normed_two, jnp.zeros((1, MODEL_WIDTH), jnp.float32)], axis=0)
    expert_inputs = padded[slot_owner].reshape(E, CAP, MODEL_WIDTH)
    gate_act = low_back(jnp.einsum('ecd,edh->ech', expert_inputs, w_gate, precision=highest_precision))
    up_act = low_back(jnp.einsum('ecd,edh->ech', expert_inputs, w_up, precision=highest_precision))
    inner_act = low(jax.nn.silu(gate_act) * up_act)
    expert_out = low_back(jnp.einsum('ech,ehd->ecd', inner_act, w_down, precision=highest_precision)).reshape(E * CAP, MODEL_WIDTH)
    picked = expert_out[slot_flat].reshape(token_count, TOP, MODEL_WIDTH)
    return hidden + lax.optimization_barrier(jnp.sum(gate_weights[:, :, None] * picked, axis=1))

def reference(activations, cotangent, gain_one, gain_two, w_query, key_projection_weight, value_projection_weight, w_out, w_router, w_gate, w_up, w_down, routes, doc_lengths):
    inputs_f = activations.astype(jnp.float32)
    weights = tuple((arr.astype(jnp.float32) for arr in (gain_one, gain_two, w_query, key_projection_weight, value_projection_weight, w_out, w_router, w_gate, w_up, w_down)))
    route_groups = routes.reshape(N_DP, TOK_GROUP, TOP)
    length_groups = doc_lengths.reshape(N_DP, SEQ_GROUP, DOCS)

    def forward(all_rows, weight_set):

        def scan_step(carried, group_items):
            row_block, route_rows, sequence_lengths = group_items
            return (carried, jax.checkpoint(layer_group)(row_block, route_rows, sequence_lengths, weight_set))
        _, outputs = lax.scan(scan_step, jnp.zeros((), jnp.float32), (all_rows.reshape(N_DP, TOK_GROUP, MODEL_WIDTH), route_groups, length_groups))
        return outputs.reshape(TOKENS, MODEL_WIDTH)
    result, pullback = jax.vjp(forward, inputs_f, weights)
    input_grads, weight_grads = pullback(cotangent.astype(jnp.float32))
    return (result.astype(jnp.bfloat16), input_grads.astype(jnp.bfloat16), weight_grads[0], weight_grads[1], weight_grads[2], weight_grads[3], weight_grads[4], weight_grads[5], weight_grads[6], weight_grads[7], weight_grads[8], weight_grads[9])
```

```python
import jax
import jax.numpy as jnp
from jax import lax
from jax.sharding import PartitionSpec as P

MODEL_WIDTH = 1536
HEAD_SIZE = 64
SEQUENCE_LENGTH = 1024
epsilon = 1e-06
f32 = jnp.float32
bf16 = jnp.bfloat16


def swap(block, axis, bit):
    size = lax.axis_size(axis)
    return lax.ppermute(block, axis, [(i, i ^ bit) for i in range(size)])


def bits_down(size):
    return [1 << i for i in reversed(range((size - 1).bit_length()))]


def gather_col(block):
    size = lax.axis_size("col")
    blocks = {0: block}
    for bit in bits_down(size):
        for k in sorted(blocks):
            blocks[k | bit] = swap(blocks[k], "col", bit)
    return [blocks[k] for k in range(size)]


def sum_col(parts, send_dtype=bf16):
    size = lax.axis_size("col")
    parts = dict(enumerate(parts))
    for bit in reversed(bits_down(size)):
        for k in sorted(parts):
            if k & bit:
                arrived = swap(parts.pop(k).astype(send_dtype), "col", bit)
                parts[k ^ bit] = parts[k ^ bit] + arrived.astype(f32)
    return parts[0]


def shift_row(block, step):
    size = lax.axis_size("row")
    return lax.ppermute(block, "row", [(i, (i + step) % size) for i in range(size)])


def gather_row_line(block):
    size = lax.axis_size("row")
    row = lax.axis_index("row")
    from_left, from_right = [block], [block]
    for k in range(1, size):
        from_left.append(
            lax.ppermute(from_left[-1], "row", [(i, i + 1) for i in range(k - 1, size - 1)])
        )
        from_right.append(
            lax.ppermute(from_right[-1], "row", [(i + 1, i) for i in range(0, size - k)])
        )
    return [block] + [
        jnp.where(row >= k, from_left[k], from_right[size - k]) for k in range(1, size)
    ]


def sum_dp(block, dimension):
    size = lax.axis_size("dp")
    index = lax.axis_index("dp")
    part = block.shape[dimension] // size

    def piece(owner):
        return lax.dynamic_slice_in_dim(block, owner * part, part, dimension)

    total = piece(index).astype(f32)
    for step in range(1, size):
        arrived = lax.ppermute(
            piece(lax.rem(index + step, size)),
            "dp",
            [(i, (i + step) % size) for i in range(size)],
        )
        total = total + arrived.astype(f32)
    return total.astype(bf16)


def rotation_tables(positions):
    half_width = HEAD_SIZE // 2
    frequency = 10000.0 ** (-jnp.arange(half_width).astype(f32) / half_width)
    angles = positions.astype(f32)[:, None] * frequency[None, :]
    return (jnp.cos(angles)[:, None, :], jnp.sin(angles)[:, None, :])


def rotate(values_in, cosine, sine_part, direction):
    half_width = HEAD_SIZE // 2
    first_half = values_in[..., :half_width]
    second = values_in[..., half_width:]
    return jnp.concatenate(
        [
            first_half * cosine - direction * second * sine_part,
            second * cosine + direction * first_half * sine_part,
        ],
        axis=-1,
    )


def doc_mask(sequence_lengths):
    positions = jnp.arange(SEQUENCE_LENGTH)
    doc_ends = jnp.cumsum(sequence_lengths)
    doc_ids = jnp.sum((positions[:, None] >= doc_ends[None, :]).astype(jnp.int32), axis=1)
    return (doc_ids[:, None] == doc_ids[None, :]) & (positions[:, None] >= positions[None, :])


def score_block(query_matrix, projected_keys, sequence_lengths):
    local_kv = projected_keys.shape[1] // HEAD_SIZE
    grouped_queries = query_matrix.reshape(SEQUENCE_LENGTH, local_kv, -1, HEAD_SIZE)
    key_heads = projected_keys.reshape(SEQUENCE_LENGTH, local_kv, HEAD_SIZE)
    scores = jnp.einsum(
        "qkgd,skd->kgqs", grouped_queries, key_heads, preferred_element_type=f32
    ) * HEAD_SIZE ** (-0.5)
    return (
        jnp.where(doc_mask(sequence_lengths)[None, None], scores, -1e30),
        grouped_queries,
        key_heads,
    )


def attend_forward(query_matrix, projected_keys, projected_values, sequence_lengths):
    scores, grouped_queries, key_heads = score_block(query_matrix, projected_keys, sequence_lengths)
    top_score = jnp.max(scores, axis=-1, keepdims=True)
    expo_scores = jnp.exp(scores - top_score)
    totals = jnp.sum(expo_scores, axis=-1, keepdims=True)
    softmax_probs = (expo_scores / totals).astype(bf16)
    value_heads = projected_values.reshape(SEQUENCE_LENGTH, key_heads.shape[1], HEAD_SIZE)
    attention_output = jnp.einsum(
        "kgqs,skd->qkgd", softmax_probs, value_heads, preferred_element_type=f32
    )
    return (attention_output.reshape(SEQUENCE_LENGTH, -1), (top_score + jnp.log(totals))[..., 0])


def attend_backward(
    query_matrix, projected_keys, projected_values, sequence_lengths, log_totals, out_grad
):
    scores, grouped_queries, key_heads = score_block(query_matrix, projected_keys, sequence_lengths)
    softmax_probs = jnp.exp(scores - log_totals[..., None])
    local_kv = key_heads.shape[1]
    grad_grouped = out_grad.reshape(SEQUENCE_LENGTH, local_kv, -1, HEAD_SIZE)
    value_heads = projected_values.reshape(SEQUENCE_LENGTH, local_kv, HEAD_SIZE)
    prob_grads = jnp.einsum("qkgd,skd->kgqs", grad_grouped, value_heads, preferred_element_type=f32)
    score_grads = (
        softmax_probs * (prob_grads - jnp.sum(softmax_probs * prob_grads, axis=-1, keepdims=True))
    ).astype(bf16)
    query_grads = jnp.einsum(
        "kgqs,skd->qkgd", score_grads, key_heads, preferred_element_type=f32
    ) * HEAD_SIZE ** (-0.5)
    key_grads = jnp.einsum(
        "kgqs,qkgd->skd", score_grads, grouped_queries, preferred_element_type=f32
    ) * HEAD_SIZE ** (-0.5)
    value_grads = jnp.einsum(
        "kgqs,qkgd->skd", softmax_probs.astype(bf16), grad_grouped, preferred_element_type=f32
    )
    return (
        query_grads.reshape(SEQUENCE_LENGTH, -1),
        key_grads.reshape(SEQUENCE_LENGTH, -1),
        value_grads.reshape(SEQUENCE_LENGTH, -1),
    )


def row_totals(per_row):
    return lax.psum(per_row, "col")


def two_parts(values):
    high = values.astype(bf16)
    return jnp.concatenate([high, (values - high.astype(f32)).astype(bf16)], axis=1)


def on_device(
    activations,
    cotangent,
    gain_one,
    gain_two,
    w_query,
    key_projection_weight,
    value_projection_weight,
    w_out,
    w_router,
    w_gate,
    w_up,
    w_down,
    routes,
    doc_lengths,
):
    n_col = lax.axis_size("col")
    n_row = lax.axis_size("row")
    col = lax.axis_index("col")
    row = lax.axis_index("row")
    local_rows, width = activations.shape
    sequences = local_rows // SEQUENCE_LENGTH
    query_width = w_query.shape[1]
    kv_width = key_projection_weight.shape[1]
    qkv_width = query_width + 2 * kv_width
    local_q = query_width // HEAD_SIZE
    local_kv = kv_width // HEAD_SIZE
    expert_count = w_router.shape[1]
    own_experts = expert_count // n_col
    hidden_width = w_gate.shape[2]
    own_width = own_experts * hidden_width
    relative = [jnp.bitwise_xor(col, k) for k in range(n_col)]

    attn_weight = jnp.concatenate(
        [w_query, key_projection_weight, value_projection_weight, w_out.T], axis=1
    )
    swapped = lax.ppermute(
        attn_weight,
        ("row", "col"),
        [(r * n_col + c, c * n_col + r) for r in range(n_row) for c in range(n_col)],
    )
    attn_blocks = lax.all_gather(swapped, "row", axis=0)
    attn_rel = jnp.concatenate(
        [lax.dynamic_index_in_dim(attn_blocks, relative[k], 0, False) for k in range(n_col)], axis=0
    )
    qkv_weight = attn_rel[:, :qkv_width]
    out_weight = attn_rel[:, qkv_width:]

    gain_one_f = gain_one.astype(f32)
    gain_two_f = gain_two.astype(f32)
    inputs_f = activations.astype(f32)
    inverse_one = lax.rsqrt(
        row_totals(jnp.sum(inputs_f * inputs_f, axis=1)) / MODEL_WIDTH + epsilon
    )
    scaled_one = inputs_f * inverse_one[:, None]
    normed_one = jnp.concatenate(
        gather_col((scaled_one * gain_one_f).astype(bf16)), axis=1
    )

    w_gate, w_up, w_down, cot_held, router_held, _ = lax.optimization_barrier(
        (w_gate, w_up, w_down, cotangent, w_router, normed_one)
    )

    def expert_block(k):
        start = relative[k] * own_experts
        gate = lax.dynamic_slice_in_dim(w_gate, start, own_experts, 0)
        up = lax.dynamic_slice_in_dim(w_up, start, own_experts, 0)
        down = lax.dynamic_slice_in_dim(w_down, start, own_experts, 0)
        return (
            jnp.concatenate(
                [
                    jnp.transpose(gate, (1, 0, 2)).reshape(width, own_width),
                    jnp.transpose(up, (1, 0, 2)).reshape(width, own_width),
                ],
                axis=1,
            ),
            down.reshape(own_width, width),
        )

    held = []
    for k in range(n_col):
        block = expert_block(k)
        if k:
            block = tuple(swap(part, "col", k) for part in block)
        held.append(block)
    gate_up_weight = jnp.concatenate([part[0] for part in held], axis=0)
    down_weight = jnp.concatenate([part[1] for part in held], axis=1)
    router_weight = jnp.concatenate(gather_col(router_held), axis=0)

    def gather_tokens(block):
        return [jnp.concatenate(gather_col(part), axis=1) for part in gather_row_line(block)]

    cot_blocks = gather_tokens(cot_held)

    qkv = jnp.dot(normed_one, qkv_weight, preferred_element_type=f32)
    positions = jnp.arange(local_rows) % SEQUENCE_LENGTH
    cosine, sine_part = rotation_tables(positions)
    query_matrix = (
        rotate(qkv[:, :query_width].reshape(-1, local_q, HEAD_SIZE), cosine, sine_part, 1.0)
        .astype(bf16)
        .reshape(-1, query_width)
    )
    projected_keys = (
        rotate(
            qkv[:, query_width : query_width + kv_width].reshape(-1, local_kv, HEAD_SIZE),
            cosine,
            sine_part,
            1.0,
        )
        .astype(bf16)
        .reshape(-1, kv_width)
    )
    projected_values = qkv[:, query_width + kv_width :].astype(bf16)
    own_lengths = lax.dynamic_slice_in_dim(doc_lengths, row * sequences, sequences, 0)

    def sequence(array, s):
        return array[s * SEQUENCE_LENGTH : (s + 1) * SEQUENCE_LENGTH]

    attended, log_totals = zip(
        *[
            attend_forward(
                sequence(query_matrix, s),
                sequence(projected_keys, s),
                sequence(projected_values, s),
                own_lengths[s],
            )
            for s in range(sequences)
        ]
    )
    attended = jnp.concatenate(attended, axis=0).astype(bf16)

    def feature_parts(left, weight):
        return [
            jnp.einsum(
                "tj,dj->td", left, weight[k * width : (k + 1) * width], preferred_element_type=f32
            )
            for k in range(n_col)
        ]

    hidden = inputs_f + sum_col(feature_parts(attended, out_weight))
    inverse_two = lax.rsqrt(row_totals(jnp.sum(hidden * hidden, axis=1)) / MODEL_WIDTH + epsilon)
    scaled_two = hidden * inverse_two[:, None]
    normed_two = (scaled_two * gain_two_f).astype(bf16)
    normed_blocks = gather_tokens(normed_two)

    expert_ids = jnp.arange(expert_count)
    spread = (
        jnp.arange(own_experts)[:, None] == (jnp.arange(own_width) // hidden_width)[None, :]
    ).astype(bf16)
    spread_twice = jnp.concatenate([spread, spread], axis=0)

    mixed, token_terms, gate_terms = [], [], []
    weighted_all, grads_all = [], []
    own_gates = own_routed = None
    for k in range(n_row):
        source = lax.rem(row - k + n_row, n_row)
        block = normed_blocks[k]
        block_routes = lax.dynamic_slice_in_dim(routes, source * local_rows, local_rows, 0)
        routed = jnp.any(block_routes[:, :, None] == expert_ids[None, None, :], axis=1)
        logits = jnp.dot(block, router_weight, preferred_element_type=f32)
        logits = jnp.where(routed, logits, -1e30)
        raised = jnp.where(routed, jnp.exp(logits - jnp.max(logits, axis=1, keepdims=True)), 0.0)
        gates = raised / jnp.sum(raised, axis=1, keepdims=True)
        if k == 0:
            own_gates, own_routed = gates, routed
        gates_here = lax.dynamic_slice_in_dim(gates, col * own_experts, own_experts, 1)
        gate_wide = jnp.dot(two_parts(gates_here), spread_twice, preferred_element_type=f32)
        inner_raw = jnp.einsum("td,jd->tj", cot_blocks[k], down_weight, preferred_element_type=f32)
        gate_act = jnp.dot(block, gate_up_weight[:, :own_width], preferred_element_type=f32)
        up_act = jnp.dot(block, gate_up_weight[:, own_width:], preferred_element_type=f32)
        sigmoid_gate = jax.nn.sigmoid(gate_act)
        silu_gate = gate_act * sigmoid_gate
        inner = silu_gate * up_act
        inner_grads = gate_wide * inner_raw
        gate_terms.append(
            jnp.dot((inner * inner_raw).astype(bf16), spread.T, preferred_element_type=f32)
        )
        weighted = (gate_wide * inner).astype(bf16)
        gate_grad_act = (
            inner_grads * up_act * sigmoid_gate * (1.0 + gate_act * (1.0 - sigmoid_gate))
        ).astype(bf16)
        up_grad_act = (inner_grads * silu_gate).astype(bf16)
        both = jnp.concatenate([gate_grad_act, up_grad_act], axis=1)
        token_terms.append(sum_col(feature_parts(both, gate_up_weight)))
        weighted_all.append(weighted)
        grads_all.append(both)

    def sum_row(terms, send_dtype=bf16):
        total = terms[0]
        for k in range(1, n_row):
            total = total + shift_row(terms[k].astype(send_dtype), -k).astype(f32)
        return total

    gate_grads_here = sum_row(gate_terms, f32)
    gate_grads = lax.all_gather(gate_grads_here.T, "col", axis=0, tiled=True).T
    chosen_grads = own_gates * (
        gate_grads - jnp.sum(own_gates * gate_grads, axis=1, keepdims=True)
    )
    logit_grads = jnp.where(own_routed, chosen_grads, 0.0).astype(bf16)
    router_grad = jnp.einsum("gd,ge->ed", normed_two, logit_grads, preferred_element_type=f32)
    router_input_grads = jnp.einsum("ge,de->gd", logit_grads, w_router, preferred_element_type=f32)

    normed_two_grads = sum_row(token_terms) + router_input_grads
    grad_scaled_two = normed_two_grads * gain_two_f
    stat_two = row_totals(jnp.sum(grad_scaled_two * scaled_two, axis=1)) / MODEL_WIDTH
    hidden_grads = cotangent.astype(f32) + inverse_two[:, None] * (
        grad_scaled_two - scaled_two * stat_two[:, None]
    )
    gain_two_part = jnp.sum(normed_two_grads * scaled_two, axis=0)
    branch_grads = jnp.concatenate(gather_col(hidden_grads.astype(bf16)), axis=1)

    weighted_rows = jnp.concatenate(weighted_all, axis=0)
    down_grad = jnp.einsum(
        "tj,td->jd", weighted_rows, jnp.concatenate(cot_blocks, axis=0), preferred_element_type=f32
    ).astype(bf16)
    gate_up_grad = jnp.einsum(
        "td,tj->dj",
        jnp.concatenate(normed_blocks, axis=0),
        jnp.concatenate(grads_all, axis=0),
        preferred_element_type=f32,
    ).astype(bf16)
    mixed = [
        sum_col(
            [
                jnp.dot(
                    part, down_weight[:, k * width : (k + 1) * width], preferred_element_type=f32
                )
                for k in range(n_col)
            ]
        )
        for part in weighted_all
    ]
    block_out = (hidden + sum_row(mixed)).astype(bf16)

    gate_up_half = sum_dp(gate_up_grad.reshape(n_col, width, 2 * own_width), 1)
    half = gate_up_half.shape[1]
    down_half = jnp.transpose(
        sum_dp(down_grad.reshape(own_width, n_col, width), 2), (1, 0, 2)
    )
    gate_grad = jnp.zeros((expert_count, half, hidden_width), f32)
    up_grad = jnp.zeros((expert_count, half, hidden_width), f32)
    down_out = jnp.zeros((expert_count, hidden_width, half), f32)
    for k in range(n_col):
        both, down = gate_up_half[k], down_half[k]
        if k:
            both, down = swap(both, "col", k), swap(down, "col", k)
        start = relative[k] * own_experts
        gate_part = jnp.transpose(
            both[:, :own_width].reshape(half, own_experts, hidden_width), (1, 0, 2)
        ).astype(f32)
        up_part = jnp.transpose(
            both[:, own_width:].reshape(half, own_experts, hidden_width), (1, 0, 2)
        ).astype(f32)
        down_part = down.reshape(own_experts, hidden_width, half).astype(f32)
        gate_grad = lax.dynamic_update_slice_in_dim(gate_grad, gate_part, start, 0)
        up_grad = lax.dynamic_update_slice_in_dim(up_grad, up_part, start, 0)
        down_out = lax.dynamic_update_slice_in_dim(down_out, down_part, start, 0)

    attended_grads = jnp.dot(branch_grads, out_weight, preferred_element_type=f32).astype(bf16)
    query_grads, key_grads, value_grads = (
        jnp.concatenate(parts, axis=0)
        for parts in zip(
            *[
                attend_backward(
                    sequence(query_matrix, s),
                    sequence(projected_keys, s),
                    sequence(projected_values, s),
                    own_lengths[s],
                    log_totals[s],
                    sequence(attended_grads, s),
                )
                for s in range(sequences)
            ]
        )
    )
    query_grads = rotate(
        query_grads.reshape(-1, local_q, HEAD_SIZE), cosine, sine_part, -1.0
    ).reshape(-1, query_width)
    key_grads = rotate(key_grads.reshape(-1, local_kv, HEAD_SIZE), cosine, sine_part, -1.0).reshape(
        -1, kv_width
    )
    qkv_grads = jnp.concatenate([query_grads, key_grads, value_grads], axis=1).astype(bf16)
    normed_one_grads = sum_col(feature_parts(qkv_grads, qkv_weight))

    attn_grad = jnp.concatenate(
        [
            jnp.einsum("td,tj->dj", normed_one, qkv_grads, preferred_element_type=f32),
            jnp.einsum("td,tj->dj", branch_grads, attended, preferred_element_type=f32),
        ],
        axis=1,
    ).astype(bf16)
    attn_grad = attn_grad.reshape(n_col, width, -1)
    attn_grad = jnp.concatenate(
        [
            lax.dynamic_index_in_dim(attn_grad, jnp.bitwise_xor(col, j), 0, False)
            for j in range(n_col)
        ],
        axis=0,
    )
    attn_grad = lax.psum_scatter(attn_grad, "row", scatter_dimension=0, tiled=True)
    attn_grad = lax.ppermute(
        attn_grad,
        ("row", "col"),
        [(r * n_col + c, c * n_col + r) for r in range(n_row) for c in range(n_col)],
    )
    attn_grad = lax.psum_scatter(
        jnp.concatenate([attn_grad[:, :qkv_width], attn_grad[:, qkv_width:].T], axis=1),
        "dp",
        scatter_dimension=0,
        tiled=True,
    ).astype(f32)

    grad_scaled_one = normed_one_grads * gain_one_f
    stat_one = row_totals(jnp.sum(grad_scaled_one * scaled_one, axis=1)) / MODEL_WIDTH
    input_grad = (
        hidden_grads + inverse_one[:, None] * (grad_scaled_one - scaled_one * stat_one[:, None])
    ).astype(bf16)
    gain_one_part = jnp.sum(normed_one_grads * scaled_one, axis=0)
    sums = lax.psum(
        jnp.concatenate([gain_one_part[None], gain_two_part[None], router_grad], axis=0),
        ("dp", "row"),
    )
    router_out = lax.dynamic_slice_in_dim(sums[2:], lax.axis_index("dp") * half, half, 1).T
    return (
        block_out,
        input_grad,
        sums[0],
        sums[1],
        attn_grad[:, :query_width],
        attn_grad[:, query_width : query_width + kv_width],
        attn_grad[:, query_width + kv_width : qkv_width],
        attn_grad[:, qkv_width:],
        router_out,
        gate_grad,
        up_grad,
        down_out,
    )


def solution(mesh):
    placed = (
        P(("dp", "row"), "col"),
        P(("dp", "row"), "col"),
        P("col"),
        P("col"),
        P("col", "row"),
        P("col", "row"),
        P("col", "row"),
        P("row", "col"),
        P("col", None),
        P(None, "col", "row"),
        P(None, "col", "row"),
        P(None, "row", "col"),
        P("dp", None),
        P("dp", None),
    )
    return jax.shard_map(
        on_device,
        mesh=mesh,
        in_specs=placed,
        out_specs=(
            P(("dp", "row"), "col"),
            P(("dp", "row"), "col"),
            P("col"),
            P("col"),
            P(("col", "dp"), "row"),
            P(("col", "dp"), "row"),
            P(("col", "dp"), "row"),
            P(("row", "dp"), "col"),
            P(("col", "dp"), None),
            P(None, ("col", "dp"), "row"),
            P(None, ("col", "dp"), "row"),
            P(None, "row", ("col", "dp")),
        ),
        check_vma=False,
    )
```

```python
import jax
import jax.numpy as jnp
from jax import lax
from jax.experimental import pallas as pl
from jax.experimental.pallas import tpu as pltpu
from jax.sharding import PartitionSpec as P

MODEL_WIDTH = 1536
HEAD_SIZE = 64
SEQUENCE_LENGTH = 1024
epsilon = 1e-06
f32 = jnp.float32
bf16 = jnp.bfloat16
LANES = 128
PAIR = 2
CHUNK = 512
VMEM_LIMIT = 60 * 1024 * 1024


def swap(block, axis, bit):
    size = lax.axis_size(axis)
    return lax.ppermute(block, axis, [(i, i ^ bit) for i in range(size)])


def bits_down(size):
    return [1 << i for i in reversed(range((size - 1).bit_length()))]


def gather_col(block):
    size = lax.axis_size("col")
    blocks = {0: block}
    for bit in bits_down(size):
        for k in sorted(blocks):
            blocks[k | bit] = swap(blocks[k], "col", bit)
    return [blocks[k] for k in range(size)]


def col_stage(parts, bit):
    kept = {}
    for k in sorted(parts):
        if not k & bit:
            arrived = swap(parts[k | bit].astype(bf16), "col", bit)
            kept[k] = parts[k].astype(f32) + arrived.astype(f32)
    return kept


def sum_col(parts):
    parts = dict(enumerate(parts))
    for bit in reversed(bits_down(lax.axis_size("col"))):
        parts = col_stage(parts, bit)
    return parts[0]


def after(values, *others):
    return lax.optimization_barrier((values, others))[0]


def crossed(n_row, n_col, bit):
    return [(r * n_col + c, c * n_col + (r ^ bit)) for r in range(n_row) for c in range(n_col)]


def gather_row_line(block):
    size = lax.axis_size("row")
    row = lax.axis_index("row")
    from_left, from_right = [block], [block]
    for k in range(1, size):
        from_left.append(
            lax.ppermute(from_left[-1], "row", [(i, i + 1) for i in range(k - 1, size - 1)])
        )
        from_right.append(
            lax.ppermute(from_right[-1], "row", [(i + 1, i) for i in range(0, size - k)])
        )
    return [block] + [
        jnp.where(row >= k, from_left[k], from_right[size - k]) for k in range(1, size)
    ]


def transposed_dot(left, right):
    return lax.dot_general(left, right, (((1,), (1,)), ((), ())), preferred_element_type=f32)


def expert_kernel(n_col, own_experts, hidden_width, first, scalars, *refs):
    refs = list(refs)

    def take(count):
        return [refs.pop(0) for _ in range(count)]

    x, cot = take(n_col), take(n_col)
    mask, router = take(2)
    gate, up, down = take(n_col), take(n_col), take(n_col)
    if not first:
        take(1)
    token_out = take(n_col)
    mix_out, gate_grad_out, up_grad_out, weighted_out, gates_out, terms_out = take(6)
    token_acc, mix_acc, terms_acc = take(3)
    rows, width = x[0].shape
    step = pl.program_id(0)
    lane = lax.broadcasted_iota(jnp.int32, (CHUNK, LANES), 1)

    @pl.when(step == 0)
    def _():
        token_acc[...] = jnp.zeros_like(token_acc)
        mix_acc[...] = jnp.zeros_like(mix_acc)
        terms_acc[...] = jnp.zeros_like(terms_acc)
        for start in range(0, rows, CHUNK):
            span = slice(start, start + CHUNK)
            here = jnp.concatenate([part[span, :] for part in x], axis=1)
            logits = jnp.dot(here, router[...], preferred_element_type=f32) + mask[span, :]
            raised = jnp.exp(logits - jnp.max(logits, axis=1, keepdims=True))
            gates_out[span, :] = raised / jnp.sum(raised, axis=1, keepdims=True)

    def pair(parts, axis):
        return [jnp.concatenate([part[i] for i in range(PAIR)], axis=axis) for part in parts]

    gate_w = jnp.concatenate(pair(gate, 1), axis=0)
    up_w = jnp.concatenate(pair(up, 1), axis=0)
    down_w = jnp.concatenate(pair(down, 0), axis=1)
    own_first = scalars[1] + PAIR * step
    for start in range(0, rows, CHUNK):
        span = slice(start, start + CHUNK)
        here = jnp.concatenate([part[span, :] for part in x], axis=1)
        there = jnp.concatenate([part[span, :] for part in cot], axis=1)
        gate_act = jnp.dot(here, gate_w, preferred_element_type=f32)
        up_act = jnp.dot(here, up_w, preferred_element_type=f32)
        raw = transposed_dot(there, down_w)
        gates = gates_out[span, :]
        wide = jnp.concatenate(
            [
                jnp.broadcast_to(
                    jnp.sum(jnp.where(lane == own_first + i, gates, 0.0), axis=1, keepdims=True),
                    (CHUNK, hidden_width),
                )
                for i in range(PAIR)
            ],
            axis=1,
        )
        sigmoid_gate = 1.0 / (1.0 + jnp.exp(-gate_act))
        silu_gate = gate_act * sigmoid_gate
        inner = silu_gate * up_act
        terms = inner * raw
        found = terms_acc[span, :]
        for i in range(PAIR):
            total = jnp.sum(
                terms[:, i * hidden_width : (i + 1) * hidden_width], axis=1, keepdims=True
            )
            found = jnp.where(lane == PAIR * step + i, total, found)
        terms_acc[span, :] = found
        inner_grads = wide * raw
        weighted = (wide * inner).astype(bf16)
        gate_grad = (
            inner_grads * up_act * sigmoid_gate * (1.0 + gate_act * (1.0 - sigmoid_gate))
        ).astype(bf16)
        up_grad = (inner_grads * silu_gate).astype(bf16)
        weighted_out[span, :] = weighted
        gate_grad_out[span, :] = gate_grad
        up_grad_out[span, :] = up_grad
        token_acc[span, :] += transposed_dot(
            jnp.concatenate([gate_grad, up_grad], axis=1),
            jnp.concatenate([gate_w, up_w], axis=1),
        )
        mix_acc[span, :] += jnp.dot(weighted, down_w, preferred_element_type=f32)

    @pl.when(step == pl.num_programs(0) - 1)
    def _():
        for k in range(n_col):
            columns = slice(k * width, (k + 1) * width)
            token_out[k][...] = token_acc[:, columns].astype(bf16)
            mix_out[scalars[2 + n_col + k]] = mix_acc[:, columns].astype(bf16)
        terms_out[...] = terms_acc[...].T[: terms_out.shape[0], :]


def expert_block(source, x, cot_all, mask, router, gate, up, down, mix):
    n_col = len(x)
    rows, width = x[0].shape
    own_experts, hidden_width = gate[1].shape[0], gate[1].shape[2]
    own_width = own_experts * hidden_width
    term_rows = -(-own_experts // 8) * 8
    col = lax.axis_index("col")
    others = [jnp.bitwise_xor(col, k) for k in range(n_col)]
    scalars = jnp.stack(
        [source, col * own_experts] + [source * n_col + other for other in others] + others
    ).astype(jnp.int32)
    once = pl.Buffered(1)
    whole = pl.BlockSpec((rows, width), lambda p, s: (0, 0), pipeline_mode=once)

    def cot_spec(k):
        return pl.BlockSpec((None, rows, width), lambda p, s: (s[2 + k], 0, 0), pipeline_mode=once)

    def weight_specs(parts):
        size = (PAIR,) + parts[0].shape[1:]
        return [pl.BlockSpec(size, lambda p, s: (s[1] // PAIR + p, 0, 0))] + [
            pl.BlockSpec(size, lambda p, s: (p, 0, 0))
        ] * (n_col - 1)

    in_specs = (
        [whole] * n_col
        + [cot_spec(k) for k in range(n_col)]
        + [
            pl.BlockSpec((rows, LANES), lambda p, s: (s[0], 0), pipeline_mode=once),
            pl.BlockSpec(router.shape, lambda p, s: (0, 0), pipeline_mode=once),
        ]
        + weight_specs(gate)
        + weight_specs(up)
        + weight_specs(down)
    )
    operands = [*x, *([cot_all] * n_col), mask, router, *gate, *up, *down]
    aliases = {}
    if mix is not None:
        in_specs.append(pl.BlockSpec(memory_space=pl.ANY))
        operands.append(mix)
        aliases = {len(operands): n_col}
    pair_columns = pl.BlockSpec((rows, PAIR * hidden_width), lambda p, s: (0, p))
    out = pl.pallas_call(
        lambda *refs: expert_kernel(n_col, own_experts, hidden_width, mix is None, *refs),
        grid_spec=pltpu.PrefetchScalarGridSpec(
            num_scalar_prefetch=1,
            grid=(own_experts // PAIR,),
            in_specs=in_specs,
            out_specs=[pl.BlockSpec((rows, width), lambda p, s: (0, 0))] * n_col
            + [pl.BlockSpec((n_col, rows, width), lambda p, s: (s[0], 0, 0))]
            + [pair_columns] * 3
            + [
                pl.BlockSpec((rows, LANES), lambda p, s: (0, 0)),
                pl.BlockSpec((term_rows, rows), lambda p, s: (0, 0)),
            ],
            scratch_shapes=[pltpu.VMEM((rows, n_col * width), f32)] * 2
            + [pltpu.VMEM((rows, LANES), f32)],
        ),
        out_shape=[jax.ShapeDtypeStruct((rows, width), bf16)] * n_col
        + [jax.ShapeDtypeStruct(cot_all.shape, bf16)]
        + [jax.ShapeDtypeStruct((rows, own_width), bf16)] * 3
        + [
            jax.ShapeDtypeStruct((rows, LANES), f32),
            jax.ShapeDtypeStruct((term_rows, rows), f32),
        ],
        input_output_aliases=aliases,
        compiler_params=pltpu.CompilerParams(vmem_limit_bytes=VMEM_LIMIT),
        cost_estimate=pl.CostEstimate(
            flops=12 * rows * n_col * width * own_width,
            bytes_accessed=40 * 1024 * 1024,
            transcendentals=rows * own_width,
        ),
        name="experts",
    )(scalars, *operands)
    return out[:n_col], out[n_col], out[n_col + 1 :]


def weight_grad_kernel(n_col, n_row, n_dp, own, flip, scalars, *refs):
    lefts, rights, out = refs[:n_row], refs[n_row:-1], refs[-1]
    left = jnp.concatenate([part[...] for part in lefts], axis=0)
    hidden_width = left.shape[1] // PAIR
    if own:
        right = [
            jnp.concatenate([rights[0][scalars[1 + b * n_col + k]] for b in range(n_row)], axis=0)
            for k in range(n_col)
        ]
    else:
        right = [
            jnp.concatenate([rights[b * n_col + k][...] for b in range(n_row)], axis=0)
            for k in range(n_col)
        ]
    width = right[0].shape[1]
    part = width // n_dp
    total = lax.dot_general(
        left,
        jnp.concatenate(right, axis=1),
        (((0,), (0,)), ((), ())),
        preferred_element_type=f32,
    )
    if flip:
        total = total.T
    total = total.astype(bf16) if part % 16 == 0 else total
    for d in range(n_dp):
        place = lax.rem(d - scalars[0] + n_dp, n_dp)
        for k in range(n_col):
            span = slice(k * width + d * part, k * width + (d + 1) * part)
            for i in range(PAIR):
                units = slice(i * hidden_width, (i + 1) * hidden_width)
                piece = total[span, units] if flip else total[units, span]
                out[place, k, i] = piece.astype(bf16)


def weight_grad(lefts, rights, flip, own_experts):
    n_col, n_row, n_dp = lax.axis_size("col"), lax.axis_size("row"), lax.axis_size("dp")
    row, col = lax.axis_index("row"), lax.axis_index("col")
    rows, own_width = lefts[0].shape
    hidden_width = own_width // own_experts
    whole = not isinstance(rights, list)
    width = rights.shape[-1] if whole else rights[0].shape[-1]
    part = width // n_dp
    scalars = jnp.stack(
        [lax.axis_index("dp")]
        + [
            jnp.bitwise_xor(row, b) * n_col + jnp.bitwise_xor(col, k)
            for b in range(n_row)
            for k in range(n_col)
        ]
    ).astype(jnp.int32)
    once = pl.Buffered(1)
    if whole:
        right_specs = [pl.BlockSpec(rights.shape, lambda p, s: (0, 0, 0), pipeline_mode=once)]
        rights = [rights]
    else:
        right_specs = [
            pl.BlockSpec((rows, width), lambda p, s: (0, 0), pipeline_mode=once)
        ] * len(rights)
    tail = (part, hidden_width) if flip else (hidden_width, part)
    return pl.pallas_call(
        lambda *refs: weight_grad_kernel(n_col, n_row, n_dp, whole, flip, *refs),
        grid_spec=pltpu.PrefetchScalarGridSpec(
            num_scalar_prefetch=1,
            grid=(own_experts // PAIR,),
            in_specs=[pl.BlockSpec((rows, PAIR * hidden_width), lambda p, s: (0, p))] * n_row
            + right_specs,
            out_specs=pl.BlockSpec((n_dp, n_col, PAIR) + tail, lambda p, s: (0, 0, p, 0, 0)),
        ),
        out_shape=jax.ShapeDtypeStruct((n_dp, n_col, own_experts) + tail, bf16),
        compiler_params=pltpu.CompilerParams(vmem_limit_bytes=VMEM_LIMIT),
        cost_estimate=pl.CostEstimate(
            flops=2 * n_row * rows * n_col * width * own_width,
            bytes_accessed=20 * 1024 * 1024,
            transcendentals=0,
        ),
        name="weight_grads",
    )(scalars, *lefts, *rights)


def sum_dp(pieces):
    size = lax.axis_size("dp")
    total = pieces[0].astype(f32)
    for step in range(1, size):
        arrived = lax.ppermute(pieces[step], "dp", [(i, (i + step) % size) for i in range(size)])
        total = total + arrived.astype(f32)
    return total.astype(bf16)


def sum_all(values, axes):
    for axis in axes:
        for bit in bits_down(lax.axis_size(axis)):
            values = values + swap(values, axis, bit)
    return values


def rotation_tables(positions):
    half_width = HEAD_SIZE // 2
    frequency = 10000.0 ** (-jnp.arange(half_width).astype(f32) / half_width)
    angles = positions.astype(f32)[:, None] * frequency[None, :]
    return (jnp.cos(angles)[:, None, :], jnp.sin(angles)[:, None, :])


def rotate(values_in, cosine, sine_part, direction):
    half_width = HEAD_SIZE // 2
    first_half = values_in[..., :half_width]
    second = values_in[..., half_width:]
    return jnp.concatenate(
        [
            first_half * cosine - direction * second * sine_part,
            second * cosine + direction * first_half * sine_part,
        ],
        axis=-1,
    )


def doc_mask(sequence_lengths):
    positions = jnp.arange(SEQUENCE_LENGTH)
    doc_ends = jnp.cumsum(sequence_lengths)
    doc_ids = jnp.sum((positions[:, None] >= doc_ends[None, :]).astype(jnp.int32), axis=1)
    return (doc_ids[:, None] == doc_ids[None, :]) & (positions[:, None] >= positions[None, :])


def score_block(query_matrix, projected_keys, sequence_lengths):
    local_kv = projected_keys.shape[1] // HEAD_SIZE
    grouped_queries = query_matrix.reshape(SEQUENCE_LENGTH, local_kv, -1, HEAD_SIZE)
    key_heads = projected_keys.reshape(SEQUENCE_LENGTH, local_kv, HEAD_SIZE)
    scores = jnp.einsum(
        "qkgd,skd->kgqs", grouped_queries, key_heads, preferred_element_type=f32
    ) * HEAD_SIZE ** (-0.5)
    return (
        jnp.where(doc_mask(sequence_lengths)[None, None], scores, -1e30),
        grouped_queries,
        key_heads,
    )


def attend_forward(query_matrix, projected_keys, projected_values, sequence_lengths):
    scores, grouped_queries, key_heads = score_block(query_matrix, projected_keys, sequence_lengths)
    top_score = jnp.max(scores, axis=-1, keepdims=True)
    expo_scores = jnp.exp(scores - top_score)
    totals = jnp.sum(expo_scores, axis=-1, keepdims=True)
    softmax_probs = (expo_scores / totals).astype(bf16)
    value_heads = projected_values.reshape(SEQUENCE_LENGTH, key_heads.shape[1], HEAD_SIZE)
    attention_output = jnp.einsum(
        "kgqs,skd->qkgd", softmax_probs, value_heads, preferred_element_type=f32
    )
    return (attention_output.reshape(SEQUENCE_LENGTH, -1), (top_score + jnp.log(totals))[..., 0])


def attend_backward(
    query_matrix, projected_keys, projected_values, sequence_lengths, log_totals, out_grad
):
    scores, grouped_queries, key_heads = score_block(query_matrix, projected_keys, sequence_lengths)
    softmax_probs = jnp.exp(scores - log_totals[..., None])
    local_kv = key_heads.shape[1]
    grad_grouped = out_grad.reshape(SEQUENCE_LENGTH, local_kv, -1, HEAD_SIZE)
    value_heads = projected_values.reshape(SEQUENCE_LENGTH, local_kv, HEAD_SIZE)
    prob_grads = jnp.einsum("qkgd,skd->kgqs", grad_grouped, value_heads, preferred_element_type=f32)
    score_grads = (
        softmax_probs * (prob_grads - jnp.sum(softmax_probs * prob_grads, axis=-1, keepdims=True))
    ).astype(bf16)
    query_grads = jnp.einsum(
        "kgqs,skd->qkgd", score_grads, key_heads, preferred_element_type=f32
    ) * HEAD_SIZE ** (-0.5)
    key_grads = jnp.einsum(
        "kgqs,qkgd->skd", score_grads, grouped_queries, preferred_element_type=f32
    ) * HEAD_SIZE ** (-0.5)
    value_grads = jnp.einsum(
        "kgqs,qkgd->skd", softmax_probs.astype(bf16), grad_grouped, preferred_element_type=f32
    )
    return (
        query_grads.reshape(SEQUENCE_LENGTH, -1),
        key_grads.reshape(SEQUENCE_LENGTH, -1),
        value_grads.reshape(SEQUENCE_LENGTH, -1),
    )


def row_totals(per_row):
    return lax.psum(per_row, "col")


def on_device(
    activations,
    cotangent,
    gain_one,
    gain_two,
    w_query,
    key_projection_weight,
    value_projection_weight,
    w_out,
    w_router,
    w_gate,
    w_up,
    w_down,
    routes,
    doc_lengths,
):
    n_col = lax.axis_size("col")
    n_row = lax.axis_size("row")
    n_dp = lax.axis_size("dp")
    col = lax.axis_index("col")
    row = lax.axis_index("row")
    local_rows, width = activations.shape
    sequences = local_rows // SEQUENCE_LENGTH
    query_width = w_query.shape[1]
    kv_width = key_projection_weight.shape[1]
    local_q = query_width // HEAD_SIZE
    local_kv = kv_width // HEAD_SIZE
    expert_count = w_router.shape[1]
    own_experts = expert_count // n_col
    relative = [jnp.bitwise_xor(col, k) for k in range(n_col)]

    def all_features(blocks):
        return jnp.concatenate(
            [lax.dynamic_index_in_dim(blocks, relative[k], 0, False) for k in range(n_col)], axis=0
        )

    crossing = crossed(n_row, n_col, 0)
    qkv_crossed = lax.ppermute(
        jnp.concatenate([w_query, key_projection_weight, value_projection_weight], axis=1),
        ("row", "col"),
        crossing,
    )
    qkv_blocks = lax.all_gather(qkv_crossed, "row", axis=0)
    routed = jnp.any(routes[:, :, None] == jnp.arange(LANES)[None, None, :], axis=1)
    mask = jnp.where(routed, 0.0, -1e30).astype(f32)

    gain_one_f = gain_one.astype(f32)
    gain_two_f = gain_two.astype(f32)
    inputs_f = activations.astype(f32)
    inverse_one = lax.rsqrt(
        row_totals(jnp.sum(inputs_f * inputs_f, axis=1)) / MODEL_WIDTH + epsilon
    )
    scaled_one = inputs_f * inverse_one[:, None]
    normed_one = jnp.concatenate(gather_col((scaled_one * gain_one_f).astype(bf16)), axis=1)
    router_parts = gather_col(w_router.T)
    router_weight = jnp.concatenate(router_parts, axis=1).T
    router_weight = jnp.pad(router_weight, ((0, 0), (0, LANES - expert_count)))
    normed_one, mask, router_weight = lax.optimization_barrier((normed_one, mask, router_weight))

    def trade(weight):
        received = []
        for k in reversed(range(1, n_col)):
            block = lax.dynamic_slice_in_dim(weight, relative[k] * own_experts, own_experts, 0)
            received.insert(0, swap(block, "col", k))
        return received

    traded = [trade(weight) for weight in after((w_gate, w_up, w_down), normed_one)]
    out_crossed = lax.ppermute(after(w_out.T, normed_one), ("row", "col"), crossing)
    out_blocks = gather_row_line(out_crossed)
    qkv_blocks = after(qkv_blocks, normed_one)
    cot_all = lax.all_gather(after(cotangent, qkv_blocks), ("row", "col"), axis=0)
    qkv_weight = all_features(qkv_blocks)

    qkv = jnp.dot(normed_one, qkv_weight, preferred_element_type=f32)
    positions = jnp.arange(local_rows) % SEQUENCE_LENGTH
    cosine, sine_part = rotation_tables(positions)
    query_matrix = (
        rotate(qkv[:, :query_width].reshape(-1, local_q, HEAD_SIZE), cosine, sine_part, 1.0)
        .astype(bf16)
        .reshape(-1, query_width)
    )
    projected_keys = (
        rotate(
            qkv[:, query_width : query_width + kv_width].reshape(-1, local_kv, HEAD_SIZE),
            cosine,
            sine_part,
            1.0,
        )
        .astype(bf16)
        .reshape(-1, kv_width)
    )
    projected_values = qkv[:, query_width + kv_width :].astype(bf16)
    own_lengths = lax.dynamic_slice_in_dim(doc_lengths, row * sequences, sequences, 0)

    def sequence(array, s):
        return array[s * SEQUENCE_LENGTH : (s + 1) * SEQUENCE_LENGTH]

    attended, log_totals = zip(
        *[
            attend_forward(
                sequence(query_matrix, s),
                sequence(projected_keys, s),
                sequence(projected_values, s),
                own_lengths[s],
            )
            for s in range(sequences)
        ]
    )
    attended = jnp.concatenate(attended, axis=0).astype(bf16)

    def feature_parts(left, weight):
        return [
            jnp.einsum(
                "tj,dj->td", left, weight[k * width : (k + 1) * width], preferred_element_type=f32
            )
            for k in range(n_col)
        ]

    out_blocks = jnp.stack(after(out_blocks, attended))
    out_weight = jnp.concatenate(
        [
            lax.dynamic_index_in_dim(out_blocks, lax.rem(row - relative[k] + n_row, n_row), 0, False)
            for k in range(n_col)
        ],
        axis=0,
    )
    hidden = inputs_f + sum_col(feature_parts(attended, out_weight))
    inverse_two = lax.rsqrt(row_totals(jnp.sum(hidden * hidden, axis=1)) / MODEL_WIDTH + epsilon)
    scaled_two = hidden * inverse_two[:, None]
    normed_two = (scaled_two * gain_two_f).astype(bf16)

    from_rows = [normed_two] + [swap(normed_two, "row", k) for k in range(1, n_row)]
    top = bits_down(n_col)[0]
    traded, cot_all = after((traded, cot_all), normed_two)
    gate_parts, up_parts, down_parts = (
        [weight] + parts for weight, parts in zip((w_gate, w_up, w_down), traded)
    )
    stages = list(reversed(bits_down(n_col)))
    sums = [[] for _ in range(n_row)]

    def advance(chain):
        state, done = sums[chain], len(sums[chain]) - 1
        if done < len(stages):
            state.append(col_stage(state[-1], stages[done]))
        elif done == len(stages):
            value = state[-1][0]
            state.append({0: swap(value.astype(bf16), "row", chain) if chain else value})

    def arrived(call):
        found = []
        for chain in range(n_row):
            if chain <= call - 2 and len(sums[chain]) <= len(stages) + 1:
                advance(chain)
                found.append(sums[chain][-1])
        return found

    gate_terms, normed_blocks = [], []
    lefts = ([], [], [])
    own_gates = mix = None
    halfway = {0: swap(normed_two, "col", top)}
    for k in range(n_row):
        if k:
            halfway[k] = after(halfway[k], token_part)
        blocks = {0: from_rows[k], top: halfway[k]}
        for bit in bits_down(n_col)[1:]:
            for held in sorted(blocks):
                blocks[held | bit] = swap(blocks[held], "col", bit)
        block = [blocks[held] for held in range(n_col)]
        following = [1] if k == 0 else list(range(2, n_row)) if k == 1 else []
        for held in following:
            halfway[held] = swap(from_rows[held], "col", top)
        block = after(block, arrived(k), [from_rows[held] for held in following])
        normed_blocks.append(block)
        token_part, mix, rest = expert_block(
            jnp.bitwise_xor(row, k),
            block,
            cot_all,
            mask,
            router_weight,
            gate_parts,
            up_parts,
            down_parts,
            mix,
        )
        for left, part in zip(lefts, rest[:3]):
            left.append(part)
        if k == 0:
            own_gates = rest[3][:, :expert_count]
        gate_terms.append(swap(rest[4], "row", k) if k else rest[4])
        sums[k].append(dict(enumerate(token_part)))

    normed_parts = [part for block in normed_blocks for part in block]
    gate_sum = sum(gate_terms[: n_row - 1])
    down_pieces = weight_grad(
        after(lefts[2], arrived(n_row), gate_sum), cot_all, True, own_experts
    )
    gate_sum = gate_sum + gate_terms[-1]
    gate_pieces = weight_grad(
        after(lefts[0], arrived(n_row + 1), gate_sum, down_pieces), normed_parts, True, own_experts
    )
    gate_half = swap(gate_sum, "col", top)
    last_sums = arrived(n_row + 2)
    up_pieces = weight_grad(
        after(lefts[1], last_sums, gate_half, gate_pieces), normed_parts, True, own_experts
    )
    mixed = lax.psum_scatter(
        after(mix, last_sums), ("row", "col"), scatter_dimension=0, tiled=False
    )
    arrived(n_row + 3)
    token_sum, gate_blocks, _ = lax.optimization_barrier(
        ([state[-1][0] for state in sums], {0: gate_sum, top: gate_half}, up_pieces)
    )
    for bit in bits_down(n_col)[1:]:
        for held in sorted(gate_blocks):
            gate_blocks[held | bit] = swap(gate_blocks[held], "col", bit)
    gate_grads = jnp.zeros((expert_count, local_rows), f32)
    for k in range(n_col):
        gate_grads = lax.dynamic_update_slice_in_dim(
            gate_grads, gate_blocks[k][:own_experts], relative[k] * own_experts, 0
        )
    gate_grads = gate_grads.T
    chosen_grads = own_gates * (
        gate_grads - jnp.sum(own_gates * gate_grads, axis=1, keepdims=True)
    )
    logit_grads = chosen_grads.astype(bf16)
    router_grad = jnp.einsum("gd,ge->ed", normed_two, logit_grads, preferred_element_type=f32)
    router_input_grads = jnp.einsum("ge,de->gd", logit_grads, w_router, preferred_element_type=f32)

    normed_two_grads = sum(part.astype(f32) for part in token_sum) + router_input_grads
    grad_scaled_two = normed_two_grads * gain_two_f
    stat_two = row_totals(jnp.sum(grad_scaled_two * scaled_two, axis=1)) / MODEL_WIDTH
    hidden_grads = cotangent.astype(f32) + inverse_two[:, None] * (
        grad_scaled_two - scaled_two * stat_two[:, None]
    )
    gain_two_part = jnp.sum(normed_two_grads * scaled_two, axis=0)
    branch_grads = jnp.concatenate(gather_col(hidden_grads.astype(bf16)), axis=1)

    block_out = (hidden + mixed.astype(f32)).astype(bf16)

    half = width // n_dp

    def expert_grad(pieces):
        summed = sum_dp(pieces)
        total = jnp.zeros((expert_count,) + summed.shape[2:], f32)
        for k in range(n_col):
            part = swap(summed[k], "col", k) if k else summed[k]
            total = lax.dynamic_update_slice_in_dim(
                total, part.astype(f32), relative[k] * own_experts, 0
            )
        return total

    down_out = jnp.transpose(expert_grad(down_pieces), (0, 2, 1))
    gate_grad = expert_grad(gate_pieces)
    up_grad = expert_grad(up_pieces)

    def attn_grad(blocks):
        part = blocks.shape[1] // n_dp
        blocks = blocks.reshape(n_col, n_dp, part, -1)
        index = lax.axis_index("dp")
        summed = sum_dp(
            [
                lax.dynamic_index_in_dim(blocks, lax.rem(index + step, n_dp), 1, False)
                for step in range(n_dp)
            ]
        )
        total = 0.0
        for bit in range(n_row):
            block = lax.dynamic_index_in_dim(
                summed, jnp.bitwise_xor(jnp.bitwise_xor(row, col), bit), 0, False
            )
            total = total + lax.ppermute(
                block, ("row", "col"), crossed(n_row, n_col, bit)
            ).astype(f32)
        return total

    out_grad = attn_grad(
        jnp.stack(
            [
                jnp.einsum(
                    "tj,td->jd",
                    attended,
                    branch_grads[:, k * width : (k + 1) * width],
                    preferred_element_type=f32,
                ).astype(bf16)
                for k in range(n_col)
            ]
        )
    )

    attended_grads = jnp.dot(branch_grads, out_weight, preferred_element_type=f32).astype(bf16)
    query_grads, key_grads, value_grads = (
        jnp.concatenate(parts, axis=0)
        for parts in zip(
            *[
                attend_backward(
                    sequence(query_matrix, s),
                    sequence(projected_keys, s),
                    sequence(projected_values, s),
                    own_lengths[s],
                    log_totals[s],
                    sequence(attended_grads, s),
                )
                for s in range(sequences)
            ]
        )
    )
    query_grads = rotate(
        query_grads.reshape(-1, local_q, HEAD_SIZE), cosine, sine_part, -1.0
    ).reshape(-1, query_width)
    key_grads = rotate(key_grads.reshape(-1, local_kv, HEAD_SIZE), cosine, sine_part, -1.0).reshape(
        -1, kv_width
    )
    qkv_grads = jnp.concatenate([query_grads, key_grads, value_grads], axis=1).astype(bf16)
    normed_one_grads = sum_col(feature_parts(qkv_grads, qkv_weight))

    qkv_out = attn_grad(
        jnp.einsum("td,tj->dj", normed_one, qkv_grads, preferred_element_type=f32)
        .astype(bf16)
        .reshape(n_col, width, -1)
    )

    grad_scaled_one = normed_one_grads * gain_one_f
    stat_one = row_totals(jnp.sum(grad_scaled_one * scaled_one, axis=1)) / MODEL_WIDTH
    input_grad = (
        hidden_grads + inverse_one[:, None] * (grad_scaled_one - scaled_one * stat_one[:, None])
    ).astype(bf16)
    gain_one_part = jnp.sum(normed_one_grads * scaled_one, axis=0)
    gain_one_grad = sum_all(gain_one_part, ("row", "dp"))
    totals = sum_all(jnp.concatenate([gain_two_part[None], router_grad], axis=0), ("row", "dp"))
    router_out = lax.dynamic_slice_in_dim(totals[1:], lax.axis_index("dp") * half, half, 1).T
    return (
        block_out,
        input_grad,
        gain_one_grad,
        totals[0],
        qkv_out[:, :query_width],
        qkv_out[:, query_width : query_width + kv_width],
        qkv_out[:, query_width + kv_width :],
        out_grad,
        router_out,
        gate_grad,
        up_grad,
        down_out,
    )


def solution(mesh):
    placed = (
        P(("dp", "row"), "col"),
        P(("dp", "row"), "col"),
        P("col"),
        P("col"),
        P("col", "row"),
        P("col", "row"),
        P("col", "row"),
        P("row", "col"),
        P("col", None),
        P(None, "col", "row"),
        P(None, "col", "row"),
        P(None, "row", "col"),
        P("dp", None),
        P("dp", None),
    )
    return jax.shard_map(
        on_device,
        mesh=mesh,
        in_specs=placed,
        out_specs=(
            P(("dp", "row"), "col"),
            P(("dp", "row"), "col"),
            P("col"),
            P("col"),
            P(("col", "dp"), "row"),
            P(("col", "dp"), "row"),
            P(("col", "dp"), "row"),
            P(("row", "dp"), "col"),
            P(("col", "dp"), None),
            P(None, ("col", "dp"), "row"),
            P(None, ("col", "dp"), "row"),
            P(None, "row", ("col", "dp")),
        ),
        check_vma=False,
    )
```

```python
import jax
import jax.numpy as jnp
from jax import lax
from jax.experimental import pallas as pl
from jax.experimental.pallas import tpu as pltpu
from jax.sharding import PartitionSpec as P

MODEL_WIDTH = 1536
HEAD_SIZE = 64
SEQUENCE_LENGTH = 1024
epsilon = 1e-06
f32 = jnp.float32
bf16 = jnp.bfloat16
LANES = 128
PAIR = 2
CHUNK = 512
VMEM_LIMIT = 60 * 1024 * 1024


def swap(block, axis, bit):
    size = lax.axis_size(axis)
    return lax.ppermute(block, axis, [(i, i ^ bit) for i in range(size)])


def bits_down(size):
    return [1 << i for i in reversed(range((size - 1).bit_length()))]


def gather_col(block):
    size = lax.axis_size("col")
    blocks = {0: block}
    for bit in bits_down(size):
        for k in sorted(blocks):
            blocks[k | bit] = swap(blocks[k], "col", bit)
    return [blocks[k] for k in range(size)]


def col_stage(parts, bit):
    kept = {}
    for k in sorted(parts):
        if not k & bit:
            arrived = swap(parts[k | bit].astype(bf16), "col", bit)
            kept[k] = parts[k].astype(f32) + arrived.astype(f32)
    return kept


def sum_col(parts):
    parts = dict(enumerate(parts))
    for bit in reversed(bits_down(lax.axis_size("col"))):
        parts = col_stage(parts, bit)
    return parts[0]


def after(values, *others):
    return lax.optimization_barrier((values, others))[0]


def crossed(n_row, n_col, bit):
    return [(r * n_col + c, c * n_col + (r ^ bit)) for r in range(n_row) for c in range(n_col)]


def gather_row_line(block):
    size = lax.axis_size("row")
    row = lax.axis_index("row")
    from_left, from_right = [block], [block]
    for k in range(1, size):
        from_left.append(
            lax.ppermute(from_left[-1], "row", [(i, i + 1) for i in range(k - 1, size - 1)])
        )
        from_right.append(
            lax.ppermute(from_right[-1], "row", [(i + 1, i) for i in range(0, size - k)])
        )
    return [block] + [
        jnp.where(row >= k, from_left[k], from_right[size - k]) for k in range(1, size)
    ]


def transposed_dot(left, right):
    return lax.dot_general(left, right, (((1,), (1,)), ((), ())), preferred_element_type=f32)


def expert_kernel(n_col, own_experts, hidden_width, first, scalars, *refs):
    refs = list(refs)

    def take(count):
        return [refs.pop(0) for _ in range(count)]

    x, cot = take(n_col), take(n_col)
    routes, router = take(2)
    gate, up, down = take(n_col), take(n_col), take(n_col)
    if not first:
        take(1)
    token_out = take(n_col)
    mix_out, gate_grad_out, up_grad_out, weighted_out, gates_out, terms_out = take(6)
    token_acc, mix_acc, terms_acc = take(3)
    rows, width = x[0].shape
    step = pl.program_id(0)
    lane = lax.broadcasted_iota(jnp.int32, (CHUNK, LANES), 1)

    @pl.when(step == 0)
    def _():
        token_acc[...] = jnp.zeros_like(token_acc)
        mix_acc[...] = jnp.zeros_like(mix_acc)
        terms_acc[...] = jnp.zeros_like(terms_acc)
        for start in range(0, rows, CHUNK):
            span = slice(start, start + CHUNK)
            here = jnp.concatenate([part[span, :] for part in x], axis=1)
            logits = jnp.dot(here, router[...], preferred_element_type=f32)
            named = routes[span, :]
            routed = lane == named[:, :1]
            for i in range(1, named.shape[1]):
                routed = jnp.logical_or(routed, lane == named[:, i : i + 1])
            logits = jnp.where(routed, logits, -1e30)
            raised = jnp.exp(logits - jnp.max(logits, axis=1, keepdims=True))
            gates_out[span, :] = raised / jnp.sum(raised, axis=1, keepdims=True)

    def pair(parts, axis):
        return [jnp.concatenate([part[i] for i in range(PAIR)], axis=axis) for part in parts]

    gate_w = jnp.concatenate(pair(gate, 1), axis=0)
    up_w = jnp.concatenate(pair(up, 1), axis=0)
    down_w = jnp.concatenate(pair(down, 0), axis=1)
    own_first = scalars[1] + PAIR * step
    for start in range(0, rows, CHUNK):
        span = slice(start, start + CHUNK)
        here = jnp.concatenate([part[span, :] for part in x], axis=1)
        there = jnp.concatenate([part[span, :] for part in cot], axis=1)
        gate_act = jnp.dot(here, gate_w, preferred_element_type=f32)
        up_act = jnp.dot(here, up_w, preferred_element_type=f32)
        raw = transposed_dot(there, down_w)
        gates = gates_out[span, :]
        wide = jnp.concatenate(
            [
                jnp.broadcast_to(
                    jnp.sum(jnp.where(lane == own_first + i, gates, 0.0), axis=1, keepdims=True),
                    (CHUNK, hidden_width),
                )
                for i in range(PAIR)
            ],
            axis=1,
        )
        sigmoid_gate = 1.0 / (1.0 + jnp.exp(-gate_act))
        silu_gate = gate_act * sigmoid_gate
        inner = silu_gate * up_act
        terms = inner * raw
        found = terms_acc[span, :]
        for i in range(PAIR):
            total = jnp.sum(
                terms[:, i * hidden_width : (i + 1) * hidden_width], axis=1, keepdims=True
            )
            found = jnp.where(lane == PAIR * step + i, total, found)
        terms_acc[span, :] = found
        inner_grads = wide * raw
        weighted = (wide * inner).astype(bf16)
        gate_grad = (
            inner_grads * up_act * sigmoid_gate * (1.0 + gate_act * (1.0 - sigmoid_gate))
        ).astype(bf16)
        up_grad = (inner_grads * silu_gate).astype(bf16)
        weighted_out[span, :] = weighted
        gate_grad_out[span, :] = gate_grad
        up_grad_out[span, :] = up_grad
        token_acc[span, :] += transposed_dot(
            jnp.concatenate([gate_grad, up_grad], axis=1),
            jnp.concatenate([gate_w, up_w], axis=1),
        )
        mix_acc[span, :] += jnp.dot(weighted, down_w, preferred_element_type=f32)

    @pl.when(step == pl.num_programs(0) - 1)
    def _():
        for k in range(n_col):
            columns = slice(k * width, (k + 1) * width)
            token_out[k][...] = token_acc[:, columns].astype(bf16)
            mix_out[scalars[2 + n_col + k]] = mix_acc[:, columns].astype(bf16)
        terms_out[...] = terms_acc[...].T[: terms_out.shape[0], :]


def expert_block(source, x, cot_all, routes, router, gate, up, down, mix):
    n_col = len(x)
    rows, width = x[0].shape
    own_experts, hidden_width = gate[1].shape[0], gate[1].shape[2]
    own_width = own_experts * hidden_width
    term_rows = -(-own_experts // 8) * 8
    col = lax.axis_index("col")
    others = [jnp.bitwise_xor(col, k) for k in range(n_col)]
    scalars = jnp.stack(
        [source, col * own_experts] + [source * n_col + other for other in others] + others
    ).astype(jnp.int32)
    once = pl.Buffered(1)
    whole = pl.BlockSpec((rows, width), lambda p, s: (0, 0), pipeline_mode=once)

    def cot_spec(k):
        return pl.BlockSpec((None, rows, width), lambda p, s: (s[2 + k], 0, 0), pipeline_mode=once)

    def weight_specs(parts):
        size = (PAIR,) + parts[0].shape[1:]
        return [pl.BlockSpec(size, lambda p, s: (s[1] // PAIR + p, 0, 0))] + [
            pl.BlockSpec(size, lambda p, s: (p, 0, 0))
        ] * (n_col - 1)

    in_specs = (
        [whole] * n_col
        + [cot_spec(k) for k in range(n_col)]
        + [
            pl.BlockSpec((rows, routes.shape[1]), lambda p, s: (s[0], 0), pipeline_mode=once),
            pl.BlockSpec(router.shape, lambda p, s: (0, 0), pipeline_mode=once),
        ]
        + weight_specs(gate)
        + weight_specs(up)
        + weight_specs(down)
    )
    operands = [*x, *([cot_all] * n_col), routes, router, *gate, *up, *down]
    aliases = {}
    if mix is not None:
        in_specs.append(pl.BlockSpec(memory_space=pl.ANY))
        operands.append(mix)
        aliases = {len(operands): n_col}
    pair_columns = pl.BlockSpec((rows, PAIR * hidden_width), lambda p, s: (0, p))
    out = pl.pallas_call(
        lambda *refs: expert_kernel(n_col, own_experts, hidden_width, mix is None, *refs),
        grid_spec=pltpu.PrefetchScalarGridSpec(
            num_scalar_prefetch=1,
            grid=(own_experts // PAIR,),
            in_specs=in_specs,
            out_specs=[pl.BlockSpec((rows, width), lambda p, s: (0, 0))] * n_col
            + [pl.BlockSpec((n_col, rows, width), lambda p, s: (s[0], 0, 0))]
            + [pair_columns] * 3
            + [
                pl.BlockSpec((rows, LANES), lambda p, s: (0, 0)),
                pl.BlockSpec((term_rows, rows), lambda p, s: (0, 0)),
            ],
            scratch_shapes=[pltpu.VMEM((rows, n_col * width), f32)] * 2
            + [pltpu.VMEM((rows, LANES), f32)],
        ),
        out_shape=[jax.ShapeDtypeStruct((rows, width), bf16)] * n_col
        + [jax.ShapeDtypeStruct(cot_all.shape, bf16)]
        + [jax.ShapeDtypeStruct((rows, own_width), bf16)] * 3
        + [
            jax.ShapeDtypeStruct((rows, LANES), f32),
            jax.ShapeDtypeStruct((term_rows, rows), f32),
        ],
        input_output_aliases=aliases,
        compiler_params=pltpu.CompilerParams(vmem_limit_bytes=VMEM_LIMIT),
        cost_estimate=pl.CostEstimate(
            flops=12 * rows * n_col * width * own_width,
            bytes_accessed=40 * 1024 * 1024,
            transcendentals=rows * own_width,
        ),
        name="experts",
    )(scalars, *operands)
    return out[:n_col], out[n_col], out[n_col + 1 :]


def weight_grad_kernel(n_col, n_row, n_dp, own, flip, scalars, *refs):
    lefts, rights, out = refs[:n_row], refs[n_row:-1], refs[-1]
    left = jnp.concatenate([part[...] for part in lefts], axis=0)
    hidden_width = left.shape[1] // PAIR
    if own:
        right = [
            jnp.concatenate([rights[0][scalars[1 + b * n_col + k]] for b in range(n_row)], axis=0)
            for k in range(n_col)
        ]
    else:
        right = [
            jnp.concatenate([rights[b * n_col + k][...] for b in range(n_row)], axis=0)
            for k in range(n_col)
        ]
    width = right[0].shape[1]
    part = width // n_dp
    total = lax.dot_general(
        left,
        jnp.concatenate(right, axis=1),
        (((0,), (0,)), ((), ())),
        preferred_element_type=f32,
    )
    if flip:
        total = total.T
    total = total.astype(bf16) if part % 16 == 0 else total
    for d in range(n_dp):
        place = lax.rem(d - scalars[0] + n_dp, n_dp)
        for k in range(n_col):
            span = slice(k * width + d * part, k * width + (d + 1) * part)
            for i in range(PAIR):
                units = slice(i * hidden_width, (i + 1) * hidden_width)
                piece = total[span, units] if flip else total[units, span]
                out[place, k, i] = piece.astype(bf16)


def weight_grad(lefts, rights, flip, own_experts):
    n_col, n_row, n_dp = lax.axis_size("col"), lax.axis_size("row"), lax.axis_size("dp")
    row, col = lax.axis_index("row"), lax.axis_index("col")
    rows, own_width = lefts[0].shape
    hidden_width = own_width // own_experts
    whole = not isinstance(rights, list)
    width = rights.shape[-1] if whole else rights[0].shape[-1]
    part = width // n_dp
    scalars = jnp.stack(
        [lax.axis_index("dp")]
        + [
            jnp.bitwise_xor(row, b) * n_col + jnp.bitwise_xor(col, k)
            for b in range(n_row)
            for k in range(n_col)
        ]
    ).astype(jnp.int32)
    once = pl.Buffered(1)
    if whole:
        right_specs = [pl.BlockSpec(rights.shape, lambda p, s: (0, 0, 0), pipeline_mode=once)]
        rights = [rights]
    else:
        right_specs = [
            pl.BlockSpec((rows, width), lambda p, s: (0, 0), pipeline_mode=once)
        ] * len(rights)
    tail = (part, hidden_width) if flip else (hidden_width, part)
    return pl.pallas_call(
        lambda *refs: weight_grad_kernel(n_col, n_row, n_dp, whole, flip, *refs),
        grid_spec=pltpu.PrefetchScalarGridSpec(
            num_scalar_prefetch=1,
            grid=(own_experts // PAIR,),
            in_specs=[pl.BlockSpec((rows, PAIR * hidden_width), lambda p, s: (0, p))] * n_row
            + right_specs,
            out_specs=pl.BlockSpec((n_dp, n_col, PAIR) + tail, lambda p, s: (0, 0, p, 0, 0)),
        ),
        out_shape=jax.ShapeDtypeStruct((n_dp, n_col, own_experts) + tail, bf16),
        compiler_params=pltpu.CompilerParams(vmem_limit_bytes=VMEM_LIMIT),
        cost_estimate=pl.CostEstimate(
            flops=2 * n_row * rows * n_col * width * own_width,
            bytes_accessed=20 * 1024 * 1024,
            transcendentals=0,
        ),
        name="weight_grads",
    )(scalars, *lefts, *rights)


def send_dp(pieces):
    size = lax.axis_size("dp")
    return [pieces[0]] + [
        lax.ppermute(pieces[step], "dp", [(i, (i + step) % size) for i in range(size)])
        for step in range(1, size)
    ]


def add_up(terms):
    return sum(term.astype(f32) for term in terms).astype(bf16)


def sum_all(values, axes):
    for axis in axes:
        for bit in bits_down(lax.axis_size(axis)):
            values = values + swap(values, axis, bit)
    return values


def rotation_tables(positions):
    half_width = HEAD_SIZE // 2
    frequency = 10000.0 ** (-jnp.arange(half_width).astype(f32) / half_width)
    angles = positions.astype(f32)[:, None] * frequency[None, :]
    return (jnp.cos(angles)[:, None, :], jnp.sin(angles)[:, None, :])


def rotate(values_in, cosine, sine_part, direction):
    half_width = HEAD_SIZE // 2
    first_half = values_in[..., :half_width]
    second = values_in[..., half_width:]
    return jnp.concatenate(
        [
            first_half * cosine - direction * second * sine_part,
            second * cosine + direction * first_half * sine_part,
        ],
        axis=-1,
    )


def doc_mask(sequence_lengths):
    positions = jnp.arange(SEQUENCE_LENGTH)
    doc_ends = jnp.cumsum(sequence_lengths)
    doc_ids = jnp.sum((positions[:, None] >= doc_ends[None, :]).astype(jnp.int32), axis=1)
    return (doc_ids[:, None] == doc_ids[None, :]) & (positions[:, None] >= positions[None, :])


def score_block(query_matrix, projected_keys, sequence_lengths):
    local_kv = projected_keys.shape[1] // HEAD_SIZE
    grouped_queries = query_matrix.reshape(SEQUENCE_LENGTH, local_kv, -1, HEAD_SIZE)
    key_heads = projected_keys.reshape(SEQUENCE_LENGTH, local_kv, HEAD_SIZE)
    scores = jnp.einsum(
        "qkgd,skd->kgqs", grouped_queries, key_heads, preferred_element_type=f32
    ) * HEAD_SIZE ** (-0.5)
    return (
        jnp.where(doc_mask(sequence_lengths)[None, None], scores, -1e30),
        grouped_queries,
        key_heads,
    )


def attend_forward(query_matrix, projected_keys, projected_values, sequence_lengths):
    scores, grouped_queries, key_heads = score_block(query_matrix, projected_keys, sequence_lengths)
    top_score = jnp.max(scores, axis=-1, keepdims=True)
    expo_scores = jnp.exp(scores - top_score)
    totals = jnp.sum(expo_scores, axis=-1, keepdims=True)
    softmax_probs = (expo_scores / totals).astype(bf16)
    value_heads = projected_values.reshape(SEQUENCE_LENGTH, key_heads.shape[1], HEAD_SIZE)
    attention_output = jnp.einsum(
        "kgqs,skd->qkgd", softmax_probs, value_heads, preferred_element_type=f32
    )
    return (attention_output.reshape(SEQUENCE_LENGTH, -1), (top_score + jnp.log(totals))[..., 0])


def attend_backward(
    query_matrix, projected_keys, projected_values, sequence_lengths, log_totals, out_grad, others
):
    scores, grouped_queries, key_heads = score_block(query_matrix, projected_keys, sequence_lengths)
    softmax_probs = jnp.exp(scores - log_totals[..., None])
    local_kv = key_heads.shape[1]
    grad_grouped = out_grad.reshape(SEQUENCE_LENGTH, local_kv, -1, HEAD_SIZE)
    value_heads = projected_values.reshape(SEQUENCE_LENGTH, local_kv, HEAD_SIZE)
    prob_grads = jnp.einsum("qkgd,skd->kgqs", grad_grouped, value_heads, preferred_element_type=f32)
    score_grads = (
        softmax_probs * (prob_grads - jnp.sum(softmax_probs * prob_grads, axis=-1, keepdims=True))
    ).astype(bf16)
    score_grads = after(score_grads, others)
    query_grads = jnp.einsum(
        "kgqs,skd->qkgd", score_grads, key_heads, preferred_element_type=f32
    ) * HEAD_SIZE ** (-0.5)
    key_grads = jnp.einsum(
        "kgqs,qkgd->skd", score_grads, grouped_queries, preferred_element_type=f32
    ) * HEAD_SIZE ** (-0.5)
    value_grads = jnp.einsum(
        "kgqs,qkgd->skd", softmax_probs.astype(bf16), grad_grouped, preferred_element_type=f32
    )
    return (
        query_grads.reshape(SEQUENCE_LENGTH, -1),
        key_grads.reshape(SEQUENCE_LENGTH, -1),
        value_grads.reshape(SEQUENCE_LENGTH, -1),
    )


def row_totals(per_row):
    return lax.psum(per_row, "col")


def on_device(
    activations,
    cotangent,
    gain_one,
    gain_two,
    w_query,
    key_projection_weight,
    value_projection_weight,
    w_out,
    w_router,
    w_gate,
    w_up,
    w_down,
    routes,
    doc_lengths,
):
    n_col = lax.axis_size("col")
    n_row = lax.axis_size("row")
    n_dp = lax.axis_size("dp")
    col = lax.axis_index("col")
    row = lax.axis_index("row")
    local_rows, width = activations.shape
    sequences = local_rows // SEQUENCE_LENGTH
    query_width = w_query.shape[1]
    kv_width = key_projection_weight.shape[1]
    local_q = query_width // HEAD_SIZE
    local_kv = kv_width // HEAD_SIZE
    expert_count = w_router.shape[1]
    own_experts = expert_count // n_col
    relative = [jnp.bitwise_xor(col, k) for k in range(n_col)]

    def all_features(blocks):
        return jnp.concatenate(
            [lax.dynamic_index_in_dim(blocks, relative[k], 0, False) for k in range(n_col)], axis=0
        )

    crossing = crossed(n_row, n_col, 0)
    qkv_crossed = lax.ppermute(
        jnp.concatenate([w_query, key_projection_weight, value_projection_weight], axis=1),
        ("row", "col"),
        crossing,
    )
    out_crossed = lax.ppermute(w_out.T, ("row", "col"), crossing)
    qkv_blocks = lax.all_gather(qkv_crossed, "row", axis=0)

    gain_one_f = gain_one.astype(f32)
    gain_two_f = gain_two.astype(f32)
    inputs_f = activations.astype(f32)
    inverse_one = lax.rsqrt(
        row_totals(jnp.sum(inputs_f * inputs_f, axis=1)) / MODEL_WIDTH + epsilon
    )
    scaled_one = inputs_f * inverse_one[:, None]
    normed_local = (scaled_one * gain_one_f).astype(bf16)
    normed_one = jnp.concatenate(gather_col(normed_local), axis=1)
    router_parts = gather_col(w_router.T)
    router_weight = jnp.concatenate(router_parts, axis=1).T
    router_weight = jnp.pad(router_weight, ((0, 0), (0, LANES - expert_count)))
    normed_one, router_weight = lax.optimization_barrier((normed_one, router_weight))

    dp_index = lax.axis_index("dp")

    def send(weight, k):
        block = lax.dynamic_slice_in_dim(weight, relative[k] * own_experts, own_experts, 0)
        if k > 1:
            part = weight.shape[1] // n_dp
            block = lax.dynamic_slice_in_dim(block, dp_index * part, part, 1)
        return swap(block, "col", k)

    def complete(part):
        if n_dp != 2:
            return lax.all_gather(part, "dp", axis=1, tiled=True)
        other = swap(part, "dp", 1)
        return jnp.where(
            dp_index == 0,
            jnp.concatenate([part, other], axis=1),
            jnp.concatenate([other, part], axis=1),
        )

    held_weights = after((w_gate, w_up, w_down), normed_local)
    sent = [[send(weight, k) for k in range(2, n_col)] for weight in held_weights]
    normed_one, sent = lax.optimization_barrier((normed_one, sent))
    near = [send(weight, 1) for weight in after((w_gate, w_up, w_down), normed_one)]
    qkv_blocks = after(qkv_blocks, normed_one)
    qkv_weight = all_features(qkv_blocks)
    out_blocks = lax.all_gather(after(out_crossed, qkv_blocks), "row", axis=0)
    qkv = jnp.dot(normed_one, qkv_weight, preferred_element_type=f32)
    cot_all = lax.all_gather(after(cotangent, qkv), ("row", "col"), axis=0)
    positions = jnp.arange(local_rows) % SEQUENCE_LENGTH
    cosine, sine_part = rotation_tables(positions)
    query_matrix = (
        rotate(qkv[:, :query_width].reshape(-1, local_q, HEAD_SIZE), cosine, sine_part, 1.0)
        .astype(bf16)
        .reshape(-1, query_width)
    )
    projected_keys = (
        rotate(
            qkv[:, query_width : query_width + kv_width].reshape(-1, local_kv, HEAD_SIZE),
            cosine,
            sine_part,
            1.0,
        )
        .astype(bf16)
        .reshape(-1, kv_width)
    )
    projected_values = qkv[:, query_width + kv_width :].astype(bf16)
    own_lengths = lax.dynamic_slice_in_dim(doc_lengths, row * sequences, sequences, 0)

    def sequence(array, s):
        return array[s * SEQUENCE_LENGTH : (s + 1) * SEQUENCE_LENGTH]

    attended, log_totals = zip(
        *[
            attend_forward(
                sequence(query_matrix, s),
                sequence(projected_keys, s),
                sequence(projected_values, s),
                own_lengths[s],
            )
            for s in range(sequences)
        ]
    )
    attended = jnp.concatenate(attended, axis=0).astype(bf16)

    def feature_parts(left, weight):
        return [
            jnp.einsum(
                "tj,dj->td", left, weight[k * width : (k + 1) * width], preferred_element_type=f32
            )
            for k in range(n_col)
        ]

    far = [[complete(part) for part in parts] for parts in sent]
    attended = after(attended, far[0])
    out_weight = all_features(after(out_blocks, attended))
    hidden = inputs_f + sum_col(feature_parts(attended, out_weight))
    hidden = after(hidden, far[1])
    inverse_two = lax.rsqrt(row_totals(jnp.sum(hidden * hidden, axis=1)) / MODEL_WIDTH + epsilon)
    scaled_two = hidden * inverse_two[:, None]
    normed_two = (scaled_two * gain_two_f).astype(bf16)

    from_rows = [normed_two] + [swap(normed_two, "row", k) for k in range(1, n_row)]
    top = bits_down(n_col)[0]
    near, far, cot_all = after((near, far, cot_all), normed_two)
    gate_parts, up_parts, down_parts = (
        [weight, first] + parts
        for weight, first, parts in zip((w_gate, w_up, w_down), near, far)
    )
    stages = list(reversed(bits_down(n_col)))
    sums = [[] for _ in range(n_row)]

    def advance(chain):
        state, done = sums[chain], len(sums[chain]) - 1
        if done < len(stages):
            state.append(col_stage(state[-1], stages[done]))
        elif done == len(stages):
            value = state[-1][0]
            state.append({0: swap(value.astype(bf16), "row", chain) if chain else value})

    def arrived(call):
        found = []
        for chain in range(n_row):
            if chain <= call - 2 and len(sums[chain]) <= len(stages) + 1:
                advance(chain)
                found.append(sums[chain][-1])
        return found

    gate_terms, normed_blocks = [], []
    lefts = ([], [], [])
    own_gates = mix = None
    halfway = {0: swap(normed_two, "col", top)}
    for k in range(n_row):
        if k:
            halfway[k] = after(halfway[k], token_part)
        blocks = {0: from_rows[k], top: halfway[k]}
        for bit in bits_down(n_col)[1:]:
            for held in sorted(blocks):
                blocks[held | bit] = swap(blocks[held], "col", bit)
        block = [blocks[held] for held in range(n_col)]
        following = [1] if k == 0 else list(range(2, n_row)) if k == 1 else []
        for held in following:
            halfway[held] = swap(from_rows[held], "col", top)
        block = after(block, arrived(k), [from_rows[held] for held in following])
        normed_blocks.append(block)
        token_part, mix, rest = expert_block(
            jnp.bitwise_xor(row, k),
            block,
            cot_all,
            routes,
            router_weight,
            gate_parts,
            up_parts,
            down_parts,
            mix,
        )
        for left, part in zip(lefts, rest[:3]):
            left.append(part)
        if k == 0:
            own_gates = rest[3][:, :expert_count]
        gate_terms.append(swap(rest[4], "row", k) if k else rest[4])
        sums[k].append(dict(enumerate(token_part)))

    normed_parts = [part for block in normed_blocks for part in block]
    gate_sum = sum(gate_terms[: n_row - 1])
    down_pieces = weight_grad(
        after(lefts[2], arrived(n_row), gate_sum), cot_all, True, own_experts
    )
    down_terms = send_dp(down_pieces)
    gate_sum = gate_sum + gate_terms[-1]
    gate_pieces = weight_grad(
        after(lefts[0], arrived(n_row + 1), gate_sum, down_pieces), normed_parts, True, own_experts
    )
    gate_pair_terms = send_dp(gate_pieces)
    gate_half = swap(gate_sum, "col", top)
    last_sums = arrived(n_row + 2)
    up_pieces = weight_grad(
        after(lefts[1], last_sums, gate_half, gate_pieces, down_terms), normed_parts, True, own_experts
    )
    up_terms = send_dp(up_pieces)
    mixed = lax.psum_scatter(
        after(mix, last_sums), ("row", "col"), scatter_dimension=0, tiled=False
    )
    arrived(n_row + 3)
    token_sum, gate_blocks, gate_pair_terms, _ = lax.optimization_barrier(
        ([state[-1][0] for state in sums], {0: gate_sum, top: gate_half}, gate_pair_terms, up_pieces)
    )
    for bit in bits_down(n_col)[1:]:
        for held in sorted(gate_blocks):
            gate_blocks[held | bit] = swap(gate_blocks[held], "col", bit)
    gate_grads = jnp.concatenate(
        [
            sum(
                jnp.where(relative[k] == owner, gate_blocks[k][:own_experts], 0.0)
                for k in range(n_col)
            )
            for owner in range(n_col)
        ],
        axis=0,
    ).T
    chosen_grads = own_gates * (
        gate_grads - jnp.sum(own_gates * gate_grads, axis=1, keepdims=True)
    )
    logit_grads = chosen_grads.astype(bf16)
    router_grad = jnp.einsum("gd,ge->ed", normed_two, logit_grads, preferred_element_type=f32)
    router_input_grads = jnp.einsum("ge,de->gd", logit_grads, w_router, preferred_element_type=f32)

    normed_two_grads = sum(part.astype(f32) for part in token_sum) + router_input_grads
    grad_scaled_two = normed_two_grads * gain_two_f
    stat_two = row_totals(jnp.sum(grad_scaled_two * scaled_two, axis=1)) / MODEL_WIDTH
    hidden_grads = cotangent.astype(f32) + inverse_two[:, None] * (
        grad_scaled_two - scaled_two * stat_two[:, None]
    )
    gain_two_part = jnp.sum(normed_two_grads * scaled_two, axis=0)
    branch_grads = jnp.concatenate(gather_col(hidden_grads.astype(bf16)), axis=1)

    block_out = (hidden + mixed.astype(f32)).astype(bf16)

    half = width // n_dp

    def expert_sums(terms):
        summed = add_up(terms)
        return [summed[0]] + [swap(summed[k], "col", k) for k in reversed(range(1, n_col))][::-1]

    def expert_grad(parts):
        total = jnp.zeros((expert_count,) + parts[0].shape[1:], f32)
        for k in range(n_col):
            total = lax.dynamic_update_slice_in_dim(
                total, parts[k].astype(f32), relative[k] * own_experts, 0
            )
        return total

    expert_parts = [expert_sums(after(terms, branch_grads)) for terms in (down_terms, gate_pair_terms)]

    def halves(blocks):
        part = blocks.shape[1] // n_dp
        blocks = blocks.reshape(n_col, n_dp, part, -1)
        return send_dp(
            [
                lax.dynamic_index_in_dim(blocks, lax.rem(dp_index + step, n_dp), 1, False)
                for step in range(n_dp)
            ]
        )

    def cross(terms):
        summed = add_up(terms)
        return [
            lax.ppermute(
                lax.dynamic_index_in_dim(
                    summed, jnp.bitwise_xor(jnp.bitwise_xor(row, col), bit), 0, False
                ),
                ("row", "col"),
                crossed(n_row, n_col, bit),
            )
            for bit in range(n_row)
        ]

    out_terms = halves(
        jnp.stack(
            [
                jnp.einsum(
                    "tj,td->jd",
                    attended,
                    branch_grads[:, k * width : (k + 1) * width],
                    preferred_element_type=f32,
                ).astype(bf16)
                for k in range(n_col)
            ]
        )
    )

    attended_grads = jnp.dot(branch_grads, out_weight, preferred_element_type=f32).astype(bf16)
    query_grads, key_grads, value_grads = (
        jnp.concatenate(parts, axis=0)
        for parts in zip(
            *[
                attend_backward(
                    sequence(query_matrix, s),
                    sequence(projected_keys, s),
                    sequence(projected_values, s),
                    own_lengths[s],
                    log_totals[s],
                    sequence(attended_grads, s),
                    (up_terms, expert_parts[0]),
                )
                for s in range(sequences)
            ]
        )
    )
    expert_parts.append(expert_sums(up_terms))
    query_grads = after(query_grads, expert_parts[1])
    out_terms = cross(after(out_terms, query_grads))
    query_grads = rotate(
        query_grads.reshape(-1, local_q, HEAD_SIZE), cosine, sine_part, -1.0
    ).reshape(-1, query_width)
    key_grads = rotate(key_grads.reshape(-1, local_kv, HEAD_SIZE), cosine, sine_part, -1.0).reshape(
        -1, kv_width
    )
    qkv_grads = jnp.concatenate([query_grads, key_grads, value_grads], axis=1).astype(bf16)
    normed_one_grads = sum_col(feature_parts(qkv_grads, qkv_weight))
    expert_parts = after(expert_parts, normed_one_grads)
    down_out = jnp.transpose(expert_grad(expert_parts[0]), (0, 2, 1))
    gate_grad = expert_grad(expert_parts[1])
    up_grad = expert_grad(expert_parts[2])

    qkv_terms = halves(
        jnp.einsum("td,tj->dj", normed_one, qkv_grads, preferred_element_type=f32)
        .astype(bf16)
        .reshape(n_col, width, -1)
    )
    qkv_out = sum(part.astype(f32) for part in cross(qkv_terms))
    out_grad = sum(part.astype(f32) for part in after(out_terms, normed_one_grads))

    grad_scaled_one = normed_one_grads * gain_one_f
    stat_one = row_totals(jnp.sum(grad_scaled_one * scaled_one, axis=1)) / MODEL_WIDTH
    input_grad = (
        hidden_grads + inverse_one[:, None] * (grad_scaled_one - scaled_one * stat_one[:, None])
    ).astype(bf16)
    gain_one_part = jnp.sum(normed_one_grads * scaled_one, axis=0)
    totals = sum_all(
        jnp.concatenate([gain_one_part[None], gain_two_part[None], router_grad], axis=0),
        ("row", "dp"),
    )
    router_out = lax.dynamic_slice_in_dim(totals[2:], dp_index * half, half, 1).T
    return (
        block_out,
        input_grad,
        totals[0],
        totals[1],
        qkv_out[:, :query_width],
        qkv_out[:, query_width : query_width + kv_width],
        qkv_out[:, query_width + kv_width :],
        out_grad,
        router_out,
        gate_grad,
        up_grad,
        down_out,
    )


def solution(mesh):
    placed = (
        P(("dp", "row"), "col"),
        P(("dp", "row"), "col"),
        P("col"),
        P("col"),
        P("col", "row"),
        P("col", "row"),
        P("col", "row"),
        P("row", "col"),
        P("col", None),
        P(None, "col", "row"),
        P(None, "col", "row"),
        P(None, "row", "col"),
        P("dp", None),
        P("dp", None),
    )
    return jax.shard_map(
        on_device,
        mesh=mesh,
        in_specs=placed,
        out_specs=(
            P(("dp", "row"), "col"),
            P(("dp", "row"), "col"),
            P("col"),
            P("col"),
            P(("col", "dp"), "row"),
            P(("col", "dp"), "row"),
            P(("col", "dp"), "row"),
            P(("row", "dp"), "col"),
            P(("col", "dp"), None),
            P(None, ("col", "dp"), "row"),
            P(None, ("col", "dp"), "row"),
            P(None, "row", ("col", "dp")),
        ),
        check_vma=False,
    )
```

```python
import jax
import jax.numpy as jnp
from jax import lax
from jax.experimental import pallas as pl
from jax.experimental.pallas import tpu as pltpu
from jax.sharding import PartitionSpec as P

MODEL_WIDTH = 1536
HEAD_SIZE = 64
SEQUENCE_LENGTH = 1024
epsilon = 1e-06
f32 = jnp.float32
bf16 = jnp.bfloat16
LANES = 128
PAIR = 2
CHUNK = 512
VMEM_LIMIT = 60 * 1024 * 1024


def swap(block, axis, bit):
    size = lax.axis_size(axis)
    return lax.ppermute(block, axis, [(i, i ^ bit) for i in range(size)])


def bits_down(size):
    return [1 << i for i in reversed(range((size - 1).bit_length()))]


def gather_col(block):
    size = lax.axis_size("col")
    blocks = {0: block}
    for bit in bits_down(size):
        for k in sorted(blocks):
            blocks[k | bit] = swap(blocks[k], "col", bit)
    return [blocks[k] for k in range(size)]


def col_stage(parts, bit):
    kept = {}
    for k in sorted(parts):
        if not k & bit:
            arrived = swap(parts[k | bit].astype(bf16), "col", bit)
            kept[k] = parts[k].astype(f32) + arrived.astype(f32)
    return kept


def sum_col(parts):
    parts = dict(enumerate(parts))
    for bit in reversed(bits_down(lax.axis_size("col"))):
        parts = col_stage(parts, bit)
    return parts[0]


def after(values, *others):
    return lax.optimization_barrier((values, others))[0]


def crossed(n_row, n_col, bit):
    return [(r * n_col + c, c * n_col + (r ^ bit)) for r in range(n_row) for c in range(n_col)]


def gather_row_line(block):
    size = lax.axis_size("row")
    row = lax.axis_index("row")
    from_left, from_right = [block], [block]
    for k in range(1, size):
        from_left.append(
            lax.ppermute(from_left[-1], "row", [(i, i + 1) for i in range(k - 1, size - 1)])
        )
        from_right.append(
            lax.ppermute(from_right[-1], "row", [(i + 1, i) for i in range(0, size - k)])
        )
    return [block] + [
        jnp.where(row >= k, from_left[k], from_right[size - k]) for k in range(1, size)
    ]


def transposed_dot(left, right):
    return lax.dot_general(left, right, (((1,), (1,)), ((), ())), preferred_element_type=f32)


def expert_kernel(n_col, own_experts, hidden_width, first, scalars, *refs):
    refs = list(refs)

    def take(count):
        return [refs.pop(0) for _ in range(count)]

    x, cot = take(n_col), take(n_col)
    routes, router = take(2)
    gate, up, down = take(n_col), take(n_col), take(n_col)
    if not first:
        take(1)
    token_out = take(n_col)
    mix_out, gate_grad_out, up_grad_out, weighted_out, gates_out, terms_out = take(6)
    token_acc, mix_acc, terms_acc = take(3)
    rows, width = x[0].shape
    step = pl.program_id(0)
    lane = lax.broadcasted_iota(jnp.int32, (CHUNK, LANES), 1)

    @pl.when(step == 0)
    def _():
        token_acc[...] = jnp.zeros_like(token_acc)
        mix_acc[...] = jnp.zeros_like(mix_acc)
        terms_acc[...] = jnp.zeros_like(terms_acc)
        for start in range(0, rows, CHUNK):
            span = slice(start, start + CHUNK)
            here = jnp.concatenate([part[span, :] for part in x], axis=1)
            logits = jnp.dot(here, router[...], preferred_element_type=f32)
            named = routes[span, :]
            routed = lane == named[:, :1]
            for i in range(1, named.shape[1]):
                routed = jnp.logical_or(routed, lane == named[:, i : i + 1])
            logits = jnp.where(routed, logits, -1e30)
            raised = jnp.exp(logits - jnp.max(logits, axis=1, keepdims=True))
            gates_out[span, :] = raised / jnp.sum(raised, axis=1, keepdims=True)

    def pair(parts, axis):
        return [jnp.concatenate([part[i] for i in range(PAIR)], axis=axis) for part in parts]

    gate_w = jnp.concatenate(pair(gate, 1), axis=0)
    up_w = jnp.concatenate(pair(up, 1), axis=0)
    down_w = jnp.concatenate(pair(down, 0), axis=1)
    own_first = scalars[1] + PAIR * step
    for start in range(0, rows, CHUNK):
        span = slice(start, start + CHUNK)
        here = jnp.concatenate([part[span, :] for part in x], axis=1)
        there = jnp.concatenate([part[span, :] for part in cot], axis=1)
        gate_act = jnp.dot(here, gate_w, preferred_element_type=f32)
        up_act = jnp.dot(here, up_w, preferred_element_type=f32)
        raw = transposed_dot(there, down_w)
        gates = gates_out[span, :]
        wide = jnp.concatenate(
            [
                jnp.broadcast_to(
                    jnp.sum(jnp.where(lane == own_first + i, gates, 0.0), axis=1, keepdims=True),
                    (CHUNK, hidden_width),
                )
                for i in range(PAIR)
            ],
            axis=1,
        )
        sigmoid_gate = 1.0 / (1.0 + jnp.exp(-gate_act))
        silu_gate = gate_act * sigmoid_gate
        inner = silu_gate * up_act
        terms = inner * raw
        found = terms_acc[span, :]
        for i in range(PAIR):
            total = jnp.sum(
                terms[:, i * hidden_width : (i + 1) * hidden_width], axis=1, keepdims=True
            )
            found = jnp.where(lane == PAIR * step + i, total, found)
        terms_acc[span, :] = found
        inner_grads = wide * raw
        weighted = (wide * inner).astype(bf16)
        gate_grad = (
            inner_grads * up_act * sigmoid_gate * (1.0 + gate_act * (1.0 - sigmoid_gate))
        ).astype(bf16)
        up_grad = (inner_grads * silu_gate).astype(bf16)
        weighted_out[span, :] = weighted
        gate_grad_out[span, :] = gate_grad
        up_grad_out[span, :] = up_grad
        token_acc[span, :] += transposed_dot(
            jnp.concatenate([gate_grad, up_grad], axis=1),
            jnp.concatenate([gate_w, up_w], axis=1),
        )
        mix_acc[span, :] += jnp.dot(weighted, down_w, preferred_element_type=f32)

    @pl.when(step == pl.num_programs(0) - 1)
    def _():
        for k in range(n_col):
            columns = slice(k * width, (k + 1) * width)
            token_out[k][...] = token_acc[:, columns].astype(bf16)
            mix_out[scalars[2 + n_col + k]] = mix_acc[:, columns].astype(bf16)
        terms_out[...] = terms_acc[...].T[: terms_out.shape[0], :]


def expert_block(source, x, cot_all, routes, router, gate, up, down, mix):
    n_col = len(x)
    rows, width = x[0].shape
    own_experts, hidden_width = gate[1].shape[0], gate[1].shape[2]
    own_width = own_experts * hidden_width
    term_rows = -(-own_experts // 8) * 8
    col = lax.axis_index("col")
    others = [jnp.bitwise_xor(col, k) for k in range(n_col)]
    scalars = jnp.stack(
        [source, col * own_experts] + [source * n_col + other for other in others] + others
    ).astype(jnp.int32)
    once = pl.Buffered(1)
    whole = pl.BlockSpec((rows, width), lambda p, s: (0, 0), pipeline_mode=once)

    def cot_spec(k):
        return pl.BlockSpec((None, rows, width), lambda p, s: (s[2 + k], 0, 0), pipeline_mode=once)

    def weight_specs(parts):
        size = (PAIR,) + parts[0].shape[1:]
        return [pl.BlockSpec(size, lambda p, s: (s[1] // PAIR + p, 0, 0))] + [
            pl.BlockSpec(size, lambda p, s: (p, 0, 0))
        ] * (n_col - 1)

    in_specs = (
        [whole] * n_col
        + [cot_spec(k) for k in range(n_col)]
        + [
            pl.BlockSpec((rows, routes.shape[1]), lambda p, s: (s[0], 0), pipeline_mode=once),
            pl.BlockSpec(router.shape, lambda p, s: (0, 0), pipeline_mode=once),
        ]
        + weight_specs(gate)
        + weight_specs(up)
        + weight_specs(down)
    )
    operands = [*x, *([cot_all] * n_col), routes, router, *gate, *up, *down]
    aliases = {}
    if mix is not None:
        in_specs.append(pl.BlockSpec(memory_space=pl.ANY))
        operands.append(mix)
        aliases = {len(operands): n_col}
    pair_columns = pl.BlockSpec((rows, PAIR * hidden_width), lambda p, s: (0, p))
    out = pl.pallas_call(
        lambda *refs: expert_kernel(n_col, own_experts, hidden_width, mix is None, *refs),
        grid_spec=pltpu.PrefetchScalarGridSpec(
            num_scalar_prefetch=1,
            grid=(own_experts // PAIR,),
            in_specs=in_specs,
            out_specs=[pl.BlockSpec((rows, width), lambda p, s: (0, 0))] * n_col
            + [pl.BlockSpec((n_col, rows, width), lambda p, s: (s[0], 0, 0))]
            + [pair_columns] * 3
            + [
                pl.BlockSpec((rows, LANES), lambda p, s: (0, 0)),
                pl.BlockSpec((term_rows, rows), lambda p, s: (0, 0)),
            ],
            scratch_shapes=[pltpu.VMEM((rows, n_col * width), f32)] * 2
            + [pltpu.VMEM((rows, LANES), f32)],
        ),
        out_shape=[jax.ShapeDtypeStruct((rows, width), bf16)] * n_col
        + [jax.ShapeDtypeStruct(cot_all.shape, bf16)]
        + [jax.ShapeDtypeStruct((rows, own_width), bf16)] * 3
        + [
            jax.ShapeDtypeStruct((rows, LANES), f32),
            jax.ShapeDtypeStruct((term_rows, rows), f32),
        ],
        input_output_aliases=aliases,
        compiler_params=pltpu.CompilerParams(vmem_limit_bytes=VMEM_LIMIT),
        cost_estimate=pl.CostEstimate(
            flops=12 * rows * n_col * width * own_width,
            bytes_accessed=40 * 1024 * 1024,
            transcendentals=rows * own_width,
        ),
        name="experts",
    )(scalars, *operands)
    return out[:n_col], out[n_col], out[n_col + 1 :]


def weight_grad_kernel(n_col, n_row, n_dp, own, flip, scalars, *refs):
    lefts, rights, out = refs[:n_row], refs[n_row:-1], refs[-1]
    left = jnp.concatenate([part[...] for part in lefts], axis=0)
    hidden_width = left.shape[1] // PAIR
    if own:
        right = [
            jnp.concatenate([rights[0][scalars[1 + b * n_col + k]] for b in range(n_row)], axis=0)
            for k in range(n_col)
        ]
    else:
        right = [
            jnp.concatenate([rights[b * n_col + k][...] for b in range(n_row)], axis=0)
            for k in range(n_col)
        ]
    width = right[0].shape[1]
    part = width // n_dp
    total = lax.dot_general(
        left,
        jnp.concatenate(right, axis=1),
        (((0,), (0,)), ((), ())),
        preferred_element_type=f32,
    )
    if flip:
        total = total.T
    total = total.astype(bf16) if part % 16 == 0 else total
    for d in range(n_dp):
        place = lax.rem(d - scalars[0] + n_dp, n_dp)
        for k in range(n_col):
            span = slice(k * width + d * part, k * width + (d + 1) * part)
            for i in range(PAIR):
                units = slice(i * hidden_width, (i + 1) * hidden_width)
                piece = total[span, units] if flip else total[units, span]
                out[place, k, i] = piece.astype(bf16)


def weight_grad(lefts, rights, flip, own_experts):
    n_col, n_row, n_dp = lax.axis_size("col"), lax.axis_size("row"), lax.axis_size("dp")
    row, col = lax.axis_index("row"), lax.axis_index("col")
    rows, own_width = lefts[0].shape
    hidden_width = own_width // own_experts
    whole = not isinstance(rights, list)
    width = rights.shape[-1] if whole else rights[0].shape[-1]
    part = width // n_dp
    scalars = jnp.stack(
        [lax.axis_index("dp")]
        + [
            jnp.bitwise_xor(row, b) * n_col + jnp.bitwise_xor(col, k)
            for b in range(n_row)
            for k in range(n_col)
        ]
    ).astype(jnp.int32)
    once = pl.Buffered(1)
    if whole:
        right_specs = [pl.BlockSpec(rights.shape, lambda p, s: (0, 0, 0), pipeline_mode=once)]
        rights = [rights]
    else:
        right_specs = [
            pl.BlockSpec((rows, width), lambda p, s: (0, 0), pipeline_mode=once)
        ] * len(rights)
    tail = (part, hidden_width) if flip else (hidden_width, part)
    return pl.pallas_call(
        lambda *refs: weight_grad_kernel(n_col, n_row, n_dp, whole, flip, *refs),
        grid_spec=pltpu.PrefetchScalarGridSpec(
            num_scalar_prefetch=1,
            grid=(own_experts // PAIR,),
            in_specs=[pl.BlockSpec((rows, PAIR * hidden_width), lambda p, s: (0, p))] * n_row
            + right_specs,
            out_specs=pl.BlockSpec((n_dp, n_col, PAIR) + tail, lambda p, s: (0, 0, p, 0, 0)),
        ),
        out_shape=jax.ShapeDtypeStruct((n_dp, n_col, own_experts) + tail, bf16),
        compiler_params=pltpu.CompilerParams(vmem_limit_bytes=VMEM_LIMIT),
        cost_estimate=pl.CostEstimate(
            flops=2 * n_row * rows * n_col * width * own_width,
            bytes_accessed=20 * 1024 * 1024,
            transcendentals=0,
        ),
        name="weight_grads",
    )(scalars, *lefts, *rights)


def send_dp(pieces):
    size = lax.axis_size("dp")
    return [pieces[0]] + [
        lax.ppermute(pieces[step], "dp", [(i, (i + step) % size) for i in range(size)])
        for step in range(1, size)
    ]


def add_up(terms):
    return sum(term.astype(f32) for term in terms).astype(bf16)


def sum_all(values, axes):
    for axis in axes:
        for bit in bits_down(lax.axis_size(axis)):
            values = values + swap(values, axis, bit)
    return values


def rotation_tables(positions):
    half_width = HEAD_SIZE // 2
    frequency = 10000.0 ** (-jnp.arange(half_width).astype(f32) / half_width)
    angles = positions.astype(f32)[:, None] * frequency[None, :]
    return (jnp.cos(angles)[:, None, :], jnp.sin(angles)[:, None, :])


def rotate(values_in, cosine, sine_part, direction):
    half_width = HEAD_SIZE // 2
    first_half = values_in[..., :half_width]
    second = values_in[..., half_width:]
    return jnp.concatenate(
        [
            first_half * cosine - direction * second * sine_part,
            second * cosine + direction * first_half * sine_part,
        ],
        axis=-1,
    )


def doc_mask(sequence_lengths):
    positions = jnp.arange(SEQUENCE_LENGTH)
    doc_ends = jnp.cumsum(sequence_lengths)
    doc_ids = jnp.sum((positions[:, None] >= doc_ends[None, :]).astype(jnp.int32), axis=1)
    return (doc_ids[:, None] == doc_ids[None, :]) & (positions[:, None] >= positions[None, :])


def score_block(query_matrix, projected_keys, sequence_lengths):
    local_kv = projected_keys.shape[1] // HEAD_SIZE
    grouped_queries = query_matrix.reshape(SEQUENCE_LENGTH, local_kv, -1, HEAD_SIZE)
    key_heads = projected_keys.reshape(SEQUENCE_LENGTH, local_kv, HEAD_SIZE)
    scores = jnp.einsum(
        "qkgd,skd->kgqs", grouped_queries, key_heads, preferred_element_type=f32
    ) * HEAD_SIZE ** (-0.5)
    return (
        jnp.where(doc_mask(sequence_lengths)[None, None], scores, -1e30),
        grouped_queries,
        key_heads,
    )


def attend_forward(query_matrix, projected_keys, projected_values, sequence_lengths):
    scores, grouped_queries, key_heads = score_block(query_matrix, projected_keys, sequence_lengths)
    top_score = jnp.max(scores, axis=-1, keepdims=True)
    expo_scores = jnp.exp(scores - top_score)
    totals = jnp.sum(expo_scores, axis=-1, keepdims=True)
    softmax_probs = (expo_scores / totals).astype(bf16)
    value_heads = projected_values.reshape(SEQUENCE_LENGTH, key_heads.shape[1], HEAD_SIZE)
    attention_output = jnp.einsum(
        "kgqs,skd->qkgd", softmax_probs, value_heads, preferred_element_type=f32
    )
    return (attention_output.reshape(SEQUENCE_LENGTH, -1), (top_score + jnp.log(totals))[..., 0])


def attend_backward(
    query_matrix, projected_keys, projected_values, sequence_lengths, log_totals, out_grad, others
):
    scores, grouped_queries, key_heads = score_block(query_matrix, projected_keys, sequence_lengths)
    softmax_probs = jnp.exp(scores - log_totals[..., None])
    local_kv = key_heads.shape[1]
    grad_grouped = out_grad.reshape(SEQUENCE_LENGTH, local_kv, -1, HEAD_SIZE)
    value_heads = projected_values.reshape(SEQUENCE_LENGTH, local_kv, HEAD_SIZE)
    prob_grads = jnp.einsum("qkgd,skd->kgqs", grad_grouped, value_heads, preferred_element_type=f32)
    score_grads = (
        softmax_probs * (prob_grads - jnp.sum(softmax_probs * prob_grads, axis=-1, keepdims=True))
    ).astype(bf16)
    score_grads = after(score_grads, others)
    query_grads = jnp.einsum(
        "kgqs,skd->qkgd", score_grads, key_heads, preferred_element_type=f32
    ) * HEAD_SIZE ** (-0.5)
    key_grads = jnp.einsum(
        "kgqs,qkgd->skd", score_grads, grouped_queries, preferred_element_type=f32
    ) * HEAD_SIZE ** (-0.5)
    value_grads = jnp.einsum(
        "kgqs,qkgd->skd", softmax_probs.astype(bf16), grad_grouped, preferred_element_type=f32
    )
    return (
        query_grads.reshape(SEQUENCE_LENGTH, -1),
        key_grads.reshape(SEQUENCE_LENGTH, -1),
        value_grads.reshape(SEQUENCE_LENGTH, -1),
    )


def row_totals(per_row):
    return lax.psum(per_row, "col")


def on_device(
    activations,
    cotangent,
    gain_one,
    gain_two,
    w_query,
    key_projection_weight,
    value_projection_weight,
    w_out,
    w_router,
    w_gate,
    w_up,
    w_down,
    routes,
    doc_lengths,
):
    n_col = lax.axis_size("col")
    n_row = lax.axis_size("row")
    n_dp = lax.axis_size("dp")
    col = lax.axis_index("col")
    row = lax.axis_index("row")
    local_rows, width = activations.shape
    sequences = local_rows // SEQUENCE_LENGTH
    query_width = w_query.shape[1]
    kv_width = key_projection_weight.shape[1]
    local_q = query_width // HEAD_SIZE
    local_kv = kv_width // HEAD_SIZE
    expert_count = w_router.shape[1]
    own_experts = expert_count // n_col
    relative = [jnp.bitwise_xor(col, k) for k in range(n_col)]

    def all_features(blocks):
        return jnp.concatenate(
            [lax.dynamic_index_in_dim(blocks, relative[k], 0, False) for k in range(n_col)], axis=0
        )

    crossing = crossed(n_row, n_col, 0)
    qkv_crossed = lax.ppermute(
        jnp.concatenate([w_query, key_projection_weight, value_projection_weight], axis=1),
        ("row", "col"),
        crossing,
    )
    out_crossed = lax.ppermute(w_out.T, ("row", "col"), crossing)
    qkv_blocks = lax.all_gather(qkv_crossed, "row", axis=0)

    gain_one_f = gain_one.astype(f32)
    gain_two_f = gain_two.astype(f32)
    inputs_f = activations.astype(f32)
    inverse_one = lax.rsqrt(
        row_totals(jnp.sum(inputs_f * inputs_f, axis=1)) / MODEL_WIDTH + epsilon
    )
    scaled_one = inputs_f * inverse_one[:, None]
    normed_local = (scaled_one * gain_one_f).astype(bf16)
    normed_one = jnp.concatenate(gather_col(normed_local), axis=1)
    router_parts = gather_col(w_router.T)
    router_weight = jnp.concatenate(router_parts, axis=1).T
    router_weight = jnp.pad(router_weight, ((0, 0), (0, LANES - expert_count)))
    normed_one, router_weight = lax.optimization_barrier((normed_one, router_weight))

    dp_index = lax.axis_index("dp")

    def send(weight, k):
        block = lax.dynamic_slice_in_dim(weight, relative[k] * own_experts, own_experts, 0)
        if k > 1:
            part = weight.shape[1] // n_dp
            block = lax.dynamic_slice_in_dim(block, dp_index * part, part, 1)
        return swap(block, "col", k)

    def complete(part):
        if n_dp != 2:
            return lax.all_gather(part, "dp", axis=1, tiled=True)
        other = swap(part, "dp", 1)
        return jnp.where(
            dp_index == 0,
            jnp.concatenate([part, other], axis=1),
            jnp.concatenate([other, part], axis=1),
        )

    held_weights = after((w_gate, w_up, w_down), normed_local)
    sent = [[send(weight, k) for k in range(2, n_col)] for weight in held_weights]
    normed_one, sent = lax.optimization_barrier((normed_one, sent))
    near = [send(weight, 1) for weight in after((w_gate, w_up, w_down), normed_one)]
    qkv_blocks = after(qkv_blocks, normed_one)
    qkv_weight = all_features(qkv_blocks)
    out_blocks = lax.all_gather(after(out_crossed, qkv_blocks), "row", axis=0)
    qkv = jnp.dot(normed_one, qkv_weight, preferred_element_type=f32)
    cot_all = lax.all_gather(after(cotangent, qkv), ("row", "col"), axis=0)
    positions = jnp.arange(local_rows) % SEQUENCE_LENGTH
    cosine, sine_part = rotation_tables(positions)
    query_matrix = (
        rotate(qkv[:, :query_width].reshape(-1, local_q, HEAD_SIZE), cosine, sine_part, 1.0)
        .astype(bf16)
        .reshape(-1, query_width)
    )
    projected_keys = (
        rotate(
            qkv[:, query_width : query_width + kv_width].reshape(-1, local_kv, HEAD_SIZE),
            cosine,
            sine_part,
            1.0,
        )
        .astype(bf16)
        .reshape(-1, kv_width)
    )
    projected_values = qkv[:, query_width + kv_width :].astype(bf16)
    own_lengths = lax.dynamic_slice_in_dim(doc_lengths, row * sequences, sequences, 0)

    def sequence(array, s):
        return array[s * SEQUENCE_LENGTH : (s + 1) * SEQUENCE_LENGTH]

    attended, log_totals = zip(
        *[
            attend_forward(
                sequence(query_matrix, s),
                sequence(projected_keys, s),
                sequence(projected_values, s),
                own_lengths[s],
            )
            for s in range(sequences)
        ]
    )
    attended = jnp.concatenate(attended, axis=0).astype(bf16)

    def feature_parts(left, weight):
        return [
            jnp.einsum(
                "tj,dj->td", left, weight[k * width : (k + 1) * width], preferred_element_type=f32
            )
            for k in range(n_col)
        ]

    far = [[complete(part) for part in parts] for parts in sent]
    attended = after(attended, far[0])
    out_weight = all_features(after(out_blocks, attended))
    hidden = inputs_f + sum_col(feature_parts(attended, out_weight))
    hidden = after(hidden, far[1])
    inverse_two = lax.rsqrt(row_totals(jnp.sum(hidden * hidden, axis=1)) / MODEL_WIDTH + epsilon)
    scaled_two = hidden * inverse_two[:, None]
    normed_two = (scaled_two * gain_two_f).astype(bf16)

    from_rows = [normed_two] + [swap(normed_two, "row", k) for k in range(1, n_row)]
    top = bits_down(n_col)[0]
    near, far, cot_all = after((near, far, cot_all), normed_two)
    gate_parts, up_parts, down_parts = (
        [weight, first] + parts
        for weight, first, parts in zip((w_gate, w_up, w_down), near, far)
    )
    stages = list(reversed(bits_down(n_col)))
    sums = [[] for _ in range(n_row)]

    def advance(chain):
        state, done = sums[chain], len(sums[chain]) - 1
        if done < len(stages):
            state.append(col_stage(state[-1], stages[done]))
        elif done == len(stages):
            value = state[-1][0]
            state.append({0: swap(value.astype(bf16), "row", chain) if chain else value})

    def arrived(call):
        found = []
        for chain in range(n_row):
            if chain <= call - 2 and len(sums[chain]) <= len(stages) + 1:
                advance(chain)
                found.append(sums[chain][-1])
        return found

    gate_terms, normed_blocks = [], []
    lefts = ([], [], [])
    own_gates = mix = None
    halfway = {0: swap(normed_two, "col", top)}
    for k in range(n_row):
        if k:
            halfway[k] = after(halfway[k], token_part)
        blocks = {0: from_rows[k], top: halfway[k]}
        for bit in bits_down(n_col)[1:]:
            for held in sorted(blocks):
                blocks[held | bit] = swap(blocks[held], "col", bit)
        block = [blocks[held] for held in range(n_col)]
        following = [1] if k == 0 else list(range(2, n_row)) if k == 1 else []
        for held in following:
            halfway[held] = swap(from_rows[held], "col", top)
        block = after(block, arrived(k), [from_rows[held] for held in following])
        normed_blocks.append(block)
        token_part, mix, rest = expert_block(
            jnp.bitwise_xor(row, k),
            block,
            cot_all,
            routes,
            router_weight,
            gate_parts,
            up_parts,
            down_parts,
            mix,
        )
        for left, part in zip(lefts, rest[:3]):
            left.append(part)
        if k == 0:
            own_gates = rest[3][:, :expert_count]
        gate_terms.append(swap(rest[4], "row", k) if k else rest[4])
        sums[k].append(dict(enumerate(token_part)))

    normed_parts = [part for block in normed_blocks for part in block]
    gate_sum = sum(gate_terms[: n_row - 1])
    down_pieces = weight_grad(
        after(lefts[2], arrived(n_row), gate_sum), cot_all, True, own_experts
    )
    down_terms = send_dp(down_pieces)
    gate_sum = gate_sum + gate_terms[-1]
    gate_pieces = weight_grad(
        after(lefts[0], arrived(n_row + 1), gate_sum, down_pieces), normed_parts, True, own_experts
    )
    gate_pair_terms = send_dp(gate_pieces)
    gate_half = swap(gate_sum, "col", top)
    last_sums = arrived(n_row + 2)
    up_pieces = weight_grad(
        after(lefts[1], last_sums, gate_half, gate_pieces, down_terms), normed_parts, True, own_experts
    )
    up_terms = send_dp(up_pieces)
    mixed = lax.psum_scatter(
        after(mix, last_sums), ("row", "col"), scatter_dimension=0, tiled=False
    )
    arrived(n_row + 3)
    token_sum, gate_blocks, gate_pair_terms, _ = lax.optimization_barrier(
        ([state[-1][0] for state in sums], {0: gate_sum, top: gate_half}, gate_pair_terms, up_pieces)
    )
    for bit in bits_down(n_col)[1:]:
        for held in sorted(gate_blocks):
            gate_blocks[held | bit] = swap(gate_blocks[held], "col", bit)
    gate_grads = jnp.concatenate(
        [
            sum(
                jnp.where(relative[k] == owner, gate_blocks[k][:own_experts], 0.0)
                for k in range(n_col)
            )
            for owner in range(n_col)
        ],
        axis=0,
    ).T
    chosen_grads = own_gates * (
        gate_grads - jnp.sum(own_gates * gate_grads, axis=1, keepdims=True)
    )
    logit_grads = chosen_grads.astype(bf16)
    router_grad = jnp.einsum("gd,ge->ed", normed_two, logit_grads, preferred_element_type=f32)
    router_input_grads = jnp.einsum("ge,de->gd", logit_grads, w_router, preferred_element_type=f32)

    normed_two_grads = sum(part.astype(f32) for part in token_sum) + router_input_grads
    grad_scaled_two = normed_two_grads * gain_two_f
    stat_two = row_totals(jnp.sum(grad_scaled_two * scaled_two, axis=1)) / MODEL_WIDTH
    hidden_grads = cotangent.astype(f32) + inverse_two[:, None] * (
        grad_scaled_two - scaled_two * stat_two[:, None]
    )
    gain_two_part = jnp.sum(normed_two_grads * scaled_two, axis=0)
    branch_grads = jnp.concatenate(gather_col(hidden_grads.astype(bf16)), axis=1)

    block_out = (hidden + mixed.astype(f32)).astype(bf16)

    half = width // n_dp

    def expert_sums(terms):
        summed = add_up(terms)
        return [summed[0]] + [swap(summed[k], "col", k) for k in reversed(range(1, n_col))][::-1]

    def expert_grad(parts):
        total = jnp.zeros((expert_count,) + parts[0].shape[1:], f32)
        for k in range(n_col):
            total = lax.dynamic_update_slice_in_dim(
                total, parts[k].astype(f32), relative[k] * own_experts, 0
            )
        return total

    expert_parts = [expert_sums(after(terms, branch_grads)) for terms in (down_terms, gate_pair_terms)]

    def halves(blocks):
        part = blocks.shape[1] // n_dp
        blocks = blocks.reshape(n_col, n_dp, part, -1)
        return send_dp(
            [
                lax.dynamic_index_in_dim(blocks, lax.rem(dp_index + step, n_dp), 1, False)
                for step in range(n_dp)
            ]
        )

    def cross(terms):
        summed = add_up(terms)
        return [
            lax.ppermute(
                lax.dynamic_index_in_dim(
                    summed, jnp.bitwise_xor(jnp.bitwise_xor(row, col), bit), 0, False
                ),
                ("row", "col"),
                crossed(n_row, n_col, bit),
            )
            for bit in range(n_row)
        ]

    out_terms = halves(
        jnp.stack(
            [
                jnp.einsum(
                    "tj,td->jd",
                    attended,
                    branch_grads[:, k * width : (k + 1) * width],
                    preferred_element_type=f32,
                ).astype(bf16)
                for k in range(n_col)
            ]
        )
    )

    attended_grads = jnp.dot(branch_grads, out_weight, preferred_element_type=f32).astype(bf16)
    query_grads, key_grads, value_grads = (
        jnp.concatenate(parts, axis=0)
        for parts in zip(
            *[
                attend_backward(
                    sequence(query_matrix, s),
                    sequence(projected_keys, s),
                    sequence(projected_values, s),
                    own_lengths[s],
                    log_totals[s],
                    sequence(attended_grads, s),
                    (up_terms, expert_parts[0], out_terms),
                )
                for s in range(sequences)
            ]
        )
    )
    expert_parts.append(expert_sums(up_terms))
    out_terms = cross(out_terms)
    query_grads = after(query_grads, expert_parts[1], out_terms)
    query_grads = rotate(
        query_grads.reshape(-1, local_q, HEAD_SIZE), cosine, sine_part, -1.0
    ).reshape(-1, query_width)
    key_grads = rotate(key_grads.reshape(-1, local_kv, HEAD_SIZE), cosine, sine_part, -1.0).reshape(
        -1, kv_width
    )
    qkv_grads = jnp.concatenate([query_grads, key_grads, value_grads], axis=1).astype(bf16)
    normed_one_grads = sum_col(feature_parts(qkv_grads, qkv_weight))
    expert_parts = after(expert_parts, normed_one_grads)
    down_out = jnp.transpose(expert_grad(expert_parts[0]), (0, 2, 1))
    gate_grad = expert_grad(expert_parts[1])
    up_grad = expert_grad(expert_parts[2])

    qkv_terms = halves(
        jnp.einsum("td,tj->dj", normed_one, qkv_grads, preferred_element_type=f32)
        .astype(bf16)
        .reshape(n_col, width, -1)
    )
    qkv_out = sum(part.astype(f32) for part in cross(qkv_terms))
    out_grad = sum(part.astype(f32) for part in after(out_terms, normed_one_grads))

    grad_scaled_one = normed_one_grads * gain_one_f
    stat_one = row_totals(jnp.sum(grad_scaled_one * scaled_one, axis=1)) / MODEL_WIDTH
    input_grad = (
        hidden_grads + inverse_one[:, None] * (grad_scaled_one - scaled_one * stat_one[:, None])
    ).astype(bf16)
    gain_one_part = jnp.sum(normed_one_grads * scaled_one, axis=0)
    totals = sum_all(
        jnp.concatenate([gain_one_part[None], gain_two_part[None], router_grad], axis=0),
        ("row", "dp"),
    )
    router_out = lax.dynamic_slice_in_dim(totals[2:], dp_index * half, half, 1).T
    return (
        block_out,
        input_grad,
        totals[0],
        totals[1],
        qkv_out[:, :query_width],
        qkv_out[:, query_width : query_width + kv_width],
        qkv_out[:, query_width + kv_width :],
        out_grad,
        router_out,
        gate_grad,
        up_grad,
        down_out,
    )


def solution(mesh):
    placed = (
        P(("dp", "row"), "col"),
        P(("dp", "row"), "col"),
        P("col"),
        P("col"),
        P("col", "row"),
        P("col", "row"),
        P("col", "row"),
        P("row", "col"),
        P("col", None),
        P(None, "col", "row"),
        P(None, "col", "row"),
        P(None, "row", "col"),
        P("dp", None),
        P("dp", None),
    )
    return jax.shard_map(
        on_device,
        mesh=mesh,
        in_specs=placed,
        out_specs=(
            P(("dp", "row"), "col"),
            P(("dp", "row"), "col"),
            P("col"),
            P("col"),
            P(("col", "dp"), "row"),
            P(("col", "dp"), "row"),
            P(("col", "dp"), "row"),
            P(("row", "dp"), "col"),
            P(("col", "dp"), None),
            P(None, ("col", "dp"), "row"),
            P(None, ("col", "dp"), "row"),
            P(None, "row", ("col", "dp")),
        ),
        check_vma=False,
    )
```
